512 devices in a mesh: seq: 64 (over y, z), kvh: 8 (over x, core).
Axes of the slice: x: 4, y: 4, z: 16, core: 2. Of those that a mesh axis runs over, the one named last changes fastest.
Arguments:
- resid: bfloat16 [64, 2, 8192], P(None, None, 'seq'), may hold values from -6 to 6
- queries: bfloat16 [64, 2, 64, 128], P(None, None, 'kvh'), may hold values from -200 to 200
- new_kv: bfloat16 [2, 64, 2, 8, 128], P(None, 'seq', None, 'kvh'), may hold values from -9 to 9
- prefix_cache: bfloat16 [2, 32768, 8, 128], P(None, 'seq', 'kvh'), may hold values from -16 to 16
- suffix_cache: bfloat16 [2, 64, 256, 8, 128], P(None, 'seq', None, 'kvh'), may hold values from -8 to 8
- suffix_lengths: int32 [64], replicated, may hold values from 1 to 256, 8192 in all
- out_weight: bfloat16 [8192, 8192], P('kvh', 'seq'), may hold values from -0.0625 to 0.0625
- norm_gain: float32 [8192], replicated, may hold values from 0.5 to 1.5
- gate_up: bfloat16 [2, 8192, 8, 3584], P(None, None, 'kvh', 'seq'), may hold values from -0.0625 to 0.0625
- down_weight: bfloat16 [28672, 8192], P('kvh', 'seq'), may hold values from -0.03125 to 0.03125
Outputs:
- layer_out: bfloat16 [64, 2, 8192], P(None, None, ('seq', 'kvh'))
The draws below stay inside these ranges and needn't reach their ends.
Inputs may be any that keep to these rules, and one draw needn't show every extreme that they name: `suffix_lengths`: the lengths sum to 8192.
All inputs are finite; a program needn't handle non-finite values.
Results may differ from the reference program's by a relative error of at most 0.02.
Values may be sent and summed in bfloat16 or wider, within the bound.
A program may use at most 128 MiB of HBM per device.

```python
import math
import jax
import jax.numpy as jnp
import numpy as np
from jax import lax

D = 8192
HEADS = 64
KVH = 8
DH = 128
FF = 28672
PRE_DEV = 512
SUF_MAX = 256
STEPS = 2
PREFIX = 32768
REQUESTS = 64
GROUP = 8
N_KVH = 8


def draw_queries(key, part):
    own_key = jax.random.fold_in(key, 11)
    normal_part = jnp.clip(jax.random.normal(own_key, (REQUESTS, STEPS, HEADS, DH), jnp.float32), -4.0, 4.0) * 3.0
    return normal_part.astype(jnp.bfloat16)


def draw_prefix_cache(key, part):
    own_key = jax.random.fold_in(key, 23)
    base = jnp.clip(jax.random.normal(own_key, (2, PREFIX, KVH, DH), jnp.float32), -6.0, 6.0)
    return base.astype(jnp.bfloat16)


def levels(stream_key, shape, pieces, least, largest):
    def one(dim, shards_of):
        heights = jax.random.uniform(jax.random.fold_in(jax.random.fold_in(stream_key, 6), dim), (shards_of,), jnp.float32, least / len(pieces), largest / len(pieces))
        return jnp.repeat(jnp.exp(heights), shape[dim] // shards_of).reshape((-1,) + (1,) * (len(shape) - dim - 1))

    factor_of = one(*pieces[0])
    for cut in pieces[1:]:
        factor_of = factor_of * one(*cut)
    return factor_of


def split_up(number_of, total, most, slope):
    loads = [(1 << 20) // math.isqrt(grade ** slope) + 1 for grade in range(2, number_of + 1)]
    spare, counts = total - most - (number_of - 1), [1] * (number_of - 1)
    while spare > 0:
        free = [i for i in range(number_of - 1) if counts[i] < most]
        whole, budget = sum([loads[i] for i in free]), spare
        for i in free:
            extra = min(most - counts[i], max(1, budget * loads[i] // whole), spare)
            counts[i] = counts[i] + extra
            spare = spare - extra
    return np.array([most] + counts)


def ragged_sizes(key, count, total, bound, skew):
    if count == 2:
        one = jax.random.randint(key, (), max(1, total - bound), min(bound, total - 1) + 1)
        return jnp.stack([one, total - one])
    tallies = jnp.asarray(split_up(count, total, bound, skew), jnp.int32)
    twos = (count - 1) // 2
    donor, sink = tallies[1:1 + 2 * twos:2], tallies[2:2 + 2 * twos:2]
    room = jnp.minimum(donor - 1, bound - sink)
    passed = jax.random.randint(jax.random.fold_in(key, 1), (twos,), 0, 1 << 20) % (room + 1)
    tallies = tallies.at[1:1 + 2 * twos:2].set(donor - passed).at[2:2 + 2 * twos:2].set(sink + passed)
    return tallies[jax.random.permutation(jax.random.fold_in(key, 2), count)]


def normal_values(rng, extent, deviation, limit, pieces=(), kind=jnp.bfloat16):
    drawn = deviation * jax.random.normal(rng, extent, jnp.float32)
    if pieces:
        drawn = drawn * levels(rng, extent, pieces, -0.22, 0.18)
    return jnp.clip(drawn, -limit, limit).astype(kind)


def setup_inputs(seed: int = 0) -> dict:
    key_of = jax.random.split(jax.random.key(seed), 11)
    resid = normal_values(key_of[0], (REQUESTS, STEPS, D), 1.0, 6.0, ((2, 64),))
    queries = draw_queries(jax.random.fold_in(key_of[10], 71), 0)
    new_kv = normal_values(key_of[2], (2, REQUESTS, STEPS, KVH, DH), 1.5, 9.0, ((1, 64), (3, 8)))
    prefix_cache = draw_prefix_cache(jax.random.fold_in(key_of[10], 71), 0)
    suffix_cache = normal_values(key_of[4], (2, REQUESTS, SUF_MAX, KVH, DH), 1.3, 8.0, ((1, 64), (3, 8)))
    suffix_lengths = ragged_sizes(key_of[5], REQUESTS, REQUESTS * SUF_MAX // 2, SUF_MAX, 2).astype(jnp.int32)
    out_weight = normal_values(key_of[6], (HEADS * DH, D), (HEADS * DH) ** -0.5, 0.0625, ((0, 8), (1, 64)))
    norm_gain = jnp.clip(1.0 + 0.1 * jax.random.normal(key_of[7], (D,), jnp.float32), 0.5, 1.5)
    gate_up = normal_values(key_of[8], (2, D, N_KVH, FF // N_KVH), D ** -0.5, 0.0625, ((2, 8), (3, 64)))
    down_weight = normal_values(key_of[9], (FF, D), FF ** -0.5, 0.03125, ((0, 8), (1, 64)))
    return {"resid": resid, "queries": queries, "new_kv": new_kv, "prefix_cache": prefix_cache, "suffix_cache": suffix_cache, "suffix_lengths": suffix_lengths, "out_weight": out_weight, "norm_gain": norm_gain, "gate_up": gate_up, "down_weight": down_weight}


theta_base = 500000.0
ntk_factor = 4.0
norm_eps = 1e-05
masked_score = -1e+30

def rotary_tables(lengths, prefix_len, head_dim, step_count):
    step_index = jnp.arange(step_count, dtype=jnp.int32)
    position = (prefix_len + lengths[:, None] + step_index[None, :]).astype(jnp.float32)
    anchor = float(prefix_len // 4)
    growth = ntk_factor * (position + 1.0) / anchor - (ntk_factor - 1.0)
    log_base = math.log(theta_base) + head_dim / (head_dim - 2.0) * jnp.log(growth)
    exponent = -2.0 * jnp.arange(head_dim // 2, dtype=jnp.float32) / head_dim
    angles = position[..., None] * jnp.exp(log_base[..., None] * exponent)
    return (jnp.cos(angles), jnp.sin(angles))

def rotate(values, cos_table, sin_table):
    half_dim = values.shape[-1] // 2
    widened = values.astype(jnp.float32)
    first_half = widened[..., :half_dim]
    second = widened[..., half_dim:]
    return jnp.concatenate([first_half * cos_table - second * sin_table, second * cos_table + first_half * sin_table], axis=-1).astype(jnp.bfloat16)

def combine(earlier, later):
    joint_peak = jnp.maximum(earlier[0], later[0])
    left_factor = jnp.exp(earlier[0] - joint_peak)
    right_factor = jnp.exp(later[0] - joint_peak)
    return (joint_peak, earlier[1] * left_factor + later[1] * right_factor, earlier[2] * left_factor[..., None] + later[2] * right_factor[..., None])

def round_wide(values):
    return lax.optimization_barrier(values.astype(jnp.bfloat16)).astype(jnp.float32)

def reference(resid, queries, new_kv, prefix_cache, suffix_cache, suffix_lengths, out_weight, norm_gain, gate_up, down_weight):
    score_scale = 1.0 / math.sqrt(DH)
    cos_table, sin_table = rotary_tables(suffix_lengths, PREFIX, DH, STEPS)
    rotated = rotate(queries, cos_table[:, :, None, :], sin_table[:, :, None, :])
    grouped = rotated.astype(jnp.float32).reshape(REQUESTS, STEPS, KVH, GROUP, DH)
    new_keys = rotate(new_kv[0], cos_table[:, :, None, :], sin_table[:, :, None, :]).astype(jnp.float32)
    new_values = new_kv[1].astype(jnp.float32)
    blocks = prefix_cache.reshape(2, PREFIX // PRE_DEV, PRE_DEV, KVH, DH).transpose(1, 0, 2, 3, 4)

    def one_block(running, prefix_block):
        scores = jnp.einsum('rtkgd,nkd->rtkgn', grouped, prefix_block[0].astype(jnp.float32)) * score_scale
        block_peak = lax.optimization_barrier(jnp.max(scores, axis=-1))
        weights = jnp.exp(scores - block_peak[..., None])
        block_total = lax.optimization_barrier(jnp.sum(weights, axis=-1))
        block_acc = jnp.einsum('rtkgn,nkd->rtkgd', round_wide(weights), prefix_block[1].astype(jnp.float32))
        return (combine(running, (block_peak, block_total, block_acc)), None)
    state_shape = (REQUESTS, STEPS, KVH, GROUP)
    initial = (jnp.full(state_shape, masked_score, jnp.float32), jnp.zeros(state_shape, jnp.float32), jnp.zeros(state_shape + (DH,), jnp.float32))
    running, _ = lax.scan(one_block, initial, blocks)
    suf_scores = jnp.einsum('rtkgd,rnkd->rtkgn', grouped, suffix_cache[0].astype(jnp.float32)) * score_scale
    suffix_live = jnp.arange(SUF_MAX, dtype=jnp.int32)[None, :] < suffix_lengths[:, None]
    suf_scores = jnp.where(suffix_live[:, None, None, None, :], suf_scores, masked_score)
    new_scores = jnp.einsum('rtkgd,rukd->rtkgu', grouped, new_keys) * score_scale
    causal = jnp.arange(STEPS, dtype=jnp.int32)[None, :] <= jnp.arange(STEPS, dtype=jnp.int32)[:, None]
    new_scores = jnp.where(causal[None, :, None, None, :], new_scores, masked_score)
    suf_peak = jnp.maximum(lax.optimization_barrier(jnp.max(suf_scores, axis=-1)), lax.optimization_barrier(jnp.max(new_scores, axis=-1)))
    suf_weights = jnp.exp(suf_scores - suf_peak[..., None])
    new_weights = jnp.exp(new_scores - suf_peak[..., None])
    suf_total = lax.optimization_barrier(jnp.sum(suf_weights, axis=-1)) + lax.optimization_barrier(jnp.sum(new_weights, axis=-1))
    suf_acc = jnp.einsum('rtkgn,rnkd->rtkgd', round_wide(suf_weights), suffix_cache[1].astype(jnp.float32))
    suf_acc = suf_acc + jnp.einsum('rtkgu,rukd->rtkgd', round_wide(new_weights), new_values)
    joint = combine(running, (suf_peak, suf_total, suf_acc))
    attention = (joint[2] / joint[1][..., None]).astype(jnp.bfloat16).reshape(REQUESTS * STEPS, HEADS * DH)
    projected = jnp.dot(attention, out_weight, preferred_element_type=jnp.float32)
    stream = (resid.reshape(REQUESTS * STEPS, D).astype(jnp.float32) + projected).astype(jnp.bfloat16)
    stream_wide = stream.astype(jnp.float32)
    inv_rms = lax.rsqrt(lax.optimization_barrier(jnp.mean(stream_wide * stream_wide, axis=-1, keepdims=True)) + norm_eps)
    normed = (stream_wide * inv_rms * norm_gain[None, :]).astype(jnp.bfloat16)
    gate_part = jnp.dot(normed, gate_up[0].reshape(D, FF), preferred_element_type=jnp.float32)
    up_part = jnp.dot(normed, gate_up[1].reshape(D, FF), preferred_element_type=jnp.float32)
    hidden = (jax.nn.silu(gate_part) * up_part).astype(jnp.bfloat16)
    ffn_part = jnp.dot(hidden, down_weight, preferred_element_type=jnp.float32)
    return (stream_wide + ffn_part).astype(jnp.bfloat16).reshape(REQUESTS, STEPS, D)
```

```python
import functools
import math

import jax
import jax.numpy as jnp
from jax import lax
from jax.experimental import pallas as pl
from jax.experimental.pallas import tpu as pltpu
from jax.sharding import PartitionSpec as P

theta_base = 500000.0
ntk_factor = 4.0
norm_eps = 1e-05
masked_score = -1e30

MESH = pl.DeviceIdType.MESH
NX, NY, NZ, NC = 4, 4, 16, 2
TOK = 128
DH = 128
HEADS = 8
PRE, SUF, NEW = 512, 256, 128
KEYS = PRE + SUF + NEW
QD = 2048
HID = 56
HPAD = 64
BF, F32 = jnp.bfloat16, jnp.float32


def rotary_tables(lengths, prefix_len, head_dim, step_count):
    step_index = jnp.arange(step_count, dtype=jnp.int32)
    position = (prefix_len + lengths[:, None] + step_index[None, :]).astype(jnp.float32)
    anchor = float(prefix_len // 4)
    growth = ntk_factor * (position + 1.0) / anchor - (ntk_factor - 1.0)
    log_base = math.log(theta_base) + head_dim / (head_dim - 2.0) * jnp.log(growth)
    exponent = -2.0 * jnp.arange(head_dim // 2, dtype=jnp.float32) / head_dim
    angles = position[..., None] * jnp.exp(log_base[..., None] * exponent)
    return (jnp.cos(angles), jnp.sin(angles))


def rotate(values, cos_table, sin_table):
    half_dim = values.shape[-1] // 2
    widened = values.astype(jnp.float32)
    first_half = widened[..., :half_dim]
    second = widened[..., half_dim:]
    return jnp.concatenate(
        [first_half * cos_table - second * sin_table, second * cos_table + first_half * sin_table],
        axis=-1,
    ).astype(jnp.bfloat16)


def dev(x, y, z, c):
    return (y * NZ + z, x * NC + c)


def kernel(
    len_ref, q_hbm, new_hbm, pre_hbm, suf_hbm, res_ref, wo_hbm, gain_hbm, wg_hbm, wd_hbm,
    out_ref,
    q_buf, k_buf, v_buf, vt_buf,
    ysend, ystat, yrecv, yrstat,
    zsend, zstat, zrecv, zrstat, att,
    wo_recv, wo_t, rs1_send, rs1_recv, res_recv,
    xt, wg_recv, wg_buf, gain_buf, gsend, grecv,
    ht, wd_recv, wd_t, rs2_send, rs2_recv, str_recv,
    loc, ssem, rsem,
):
    s = lax.axis_index("seq")
    k = lax.axis_index("kvh")
    x, c = k // NC, k % NC
    y, z = s // NZ, s % NZ

    def send(src, dst, stage, to):
        copy = pltpu.make_async_remote_copy(
            src_ref=src, dst_ref=dst, send_sem=ssem.at[stage], recv_sem=rsem.at[stage],
            device_id=to, device_id_type=MESH,
        )
        copy.start()

    def wait(ref, sem):
        pltpu.make_async_copy(ref, ref, sem).wait()

    def zpeer(i):
        return (z + 8 + ((i + 1) // 2) * (1 - 2 * (i % 2))) % NZ

    def plane_peer(i):
        return (x + i // 8) % NX, (y + (i // 2) % NY) % NY, (c + i % 2) % NC

    loads = [
        pltpu.make_async_copy(q_hbm, q_buf, loc.at[0]),
        pltpu.make_async_copy(pre_hbm.at[0], k_buf.at[pl.ds(0, PRE)], loc.at[1]),
        pltpu.make_async_copy(suf_hbm.at[0], k_buf.at[pl.ds(PRE, SUF)], loc.at[2]),
        pltpu.make_async_copy(new_hbm.at[0], k_buf.at[pl.ds(PRE + SUF, NEW)], loc.at[3]),
        pltpu.make_async_copy(pre_hbm.at[1], v_buf.at[pl.ds(0, PRE)], loc.at[4]),
        pltpu.make_async_copy(suf_hbm.at[1], v_buf.at[pl.ds(PRE, SUF)], loc.at[5]),
        pltpu.make_async_copy(new_hbm.at[1], v_buf.at[pl.ds(PRE + SUF, NEW)], loc.at[6]),
    ]
    for copy in loads:
        copy.start()
    own_wg = pltpu.make_async_copy(wg_hbm.at[:, pl.ds(pl.multiple_of(x * QD, QD), QD)], wg_recv.at[x], loc.at[7])
    own_wo = pltpu.make_async_copy(wo_hbm.at[pl.ds(pl.multiple_of(y * 256, 256), 256)], wo_recv.at[y], loc.at[8])
    own_wd = pltpu.make_async_copy(wd_hbm.at[pl.ds(pl.multiple_of(y * 896, 896), 896)], wd_recv.at[y], loc.at[9])
    own_gain = pltpu.make_async_copy(gain_hbm.at[x], gain_buf, loc.at[10])
    for copy in (own_wg, own_wo, own_wd, own_gain):
        copy.start()

    barrier = pltpu.get_barrier_semaphore()

    def greet_z(i, carry):
        pl.semaphore_signal(barrier, inc=1, device_id=dev(x, y, zpeer(i), c), device_id_type=MESH)
        return carry

    def greet_plane(i, carry):
        xp, yp, cp = plane_peer(i)
        pl.semaphore_signal(barrier, inc=1, device_id=dev(xp, yp, z, cp), device_id_type=MESH)
        return carry

    lax.fori_loop(0, NZ - 1, greet_z, 0)
    lax.fori_loop(1, 32, greet_plane, 0)

    for copy in loads:
        copy.wait()
    vt_buf[...] = v_buf[...].T
    length = len_ref[s]
    row = lax.broadcasted_iota(jnp.int32, (SUF + NEW, TOK), 0)
    lane = lax.broadcasted_iota(jnp.int32, (SUF + NEW, TOK), 1)
    live = (lane % 64 == s) & ((row < length) | ((row >= SUF) & (row - SUF <= lane // 64)))
    scale = 1.0 / math.sqrt(DH)

    def attend(dst, stat, yq):
        for h in range(2):
            qt = q_buf[yq * 2 + h]
            raw = jnp.dot(k_buf[...], qt, preferred_element_type=F32) * scale
            first = raw[:PRE]
            second = jnp.where(live, raw[PRE:], masked_score)
            peak = jnp.maximum(
                jnp.max(first, axis=0, keepdims=True), jnp.max(second, axis=0, keepdims=True)
            )
            e1 = jnp.exp(first - peak)
            e2 = jnp.exp(second - peak)
            total = jnp.sum(e1, axis=0, keepdims=True) + jnp.sum(e2, axis=0, keepdims=True)
            acc = jnp.dot(vt_buf[:, :PRE], e1.astype(BF), preferred_element_type=F32)
            acc = acc + jnp.dot(vt_buf[:, PRE:], e2.astype(BF), preferred_element_type=F32)
            dst[pl.ds(h * DH, DH)] = acc.astype(BF)
            stat[pl.ds(2 * h, 1)] = peak
            stat[pl.ds(2 * h + 1, 1)] = total

    def y_hop(d, carry):
        yp = (y + d) % NY
        attend(ysend.at[yp], ystat.at[yp], yp)
        send(ysend.at[yp], yrecv.at[y], 0, dev(x, yp, z, c))
        send(ystat.at[yp], yrstat.at[y], 1, dev(x, yp, z, c))
        return carry

    pl.semaphore_wait(barrier, 46)
    def wg_hop(d, carry):
        xp = (x + d) % NX
        send(wg_hbm.at[:, pl.ds(pl.multiple_of(xp * QD, QD), QD)], wg_recv.at[x], 8, dev(xp, y, z, c))
        return carry

    lax.fori_loop(1, NX, wg_hop, 0)
    @pl.when(x != y)
    def _():
        send(res_ref.at[pl.ds(pl.multiple_of(k * 16, 16), 16)], res_recv, 9, dev(y, x, z, c))

    @pl.when(x == y)
    def _():
        res_recv[...] = res_ref[pl.ds(pl.multiple_of(k * 16, 16), 16)]

    lax.fori_loop(1, NY, y_hop, 0)
    attend(yrecv.at[y], yrstat.at[y], y)
    wait(yrecv.at[pl.ds(0, NY - 1)], rsem.at[0])
    wait(yrstat.at[pl.ds(0, NY - 1)], rsem.at[1])

    for h in range(2):
        peaks = [yrstat[i, pl.ds(2 * h, 1)] for i in range(NY)]
        joint = functools.reduce(jnp.maximum, peaks)
        facs = [jnp.exp(p - joint) for p in peaks]
        total = sum(yrstat[i, pl.ds(2 * h + 1, 1)] * facs[i] for i in range(NY))
        acc = sum(yrecv[i, pl.ds(h * DH, DH)].astype(F32) * facs[i] for i in range(NY))
        zsend[pl.ds(h * 8, 8)] = acc.astype(BF).reshape(8, 16, TOK)
        zstat[h, pl.ds(0, 1)] = joint
        zstat[h, pl.ds(1, 1)] = total

    def z_hop(i, carry):
        zp = zpeer(i)
        send(zsend.at[zp], zrecv.at[z], 2, dev(x, y, zp, c))
        send(zstat.at[zp // 8], zrstat.at[z], 3, dev(x, y, zp, c))
        return carry

    lax.fori_loop(0, NZ - 1, z_hop, 0)

    def wy_hop(d, carry):
        yp = (y + d) % NY
        send(wo_hbm.at[pl.ds(pl.multiple_of(yp * 256, 256), 256)], wo_recv.at[y], 10, dev(x, yp, z, c))
        return carry

    def wd_hop(d, carry):
        yp = (y + d) % NY
        send(wd_hbm.at[pl.ds(pl.multiple_of(yp * 896, 896), 896)], wd_recv.at[y], 11, dev(x, yp, z, c))
        return carry

    lax.fori_loop(1, NY, wy_hop, 0)
    lax.fori_loop(1, NY, wd_hop, 0)
    zrecv[z] = zsend[z]
    zrstat[z] = zstat[z // 8]
    wait(zrecv.at[pl.ds(0, NZ - 1)], rsem.at[2])
    wait(zrstat.at[pl.ds(0, NZ - 1)], rsem.at[3])

    peaks = [zrstat[i, pl.ds(0, 1)] for i in range(NZ)]
    joint = functools.reduce(jnp.maximum, peaks)
    facs = [jnp.exp(p - joint) for p in peaks]
    total = sum(zrstat[i, pl.ds(1, 1)] * facs[i] for i in range(NZ))
    acc = sum(zrecv[i].astype(F32) * facs[i] for i in range(NZ))
    att[z] = (acc / total).astype(BF)

    def a_hop(i, carry):
        send(att.at[z], att.at[z], 4, dev(x, y, zpeer(i), c))
        return carry

    lax.fori_loop(0, NZ - 1, a_hop, 0)

    own_wo.wait()
    wait(wo_recv.at[pl.ds(0, NY - 1)], rsem.at[10])
    for i in range(NY):
        wo_t[pl.ds(i * 128, 128)] = wo_recv[i].T
    own_wg.wait()
    own_gain.wait()
    wait(wg_recv.at[pl.ds(0, NX - 1)], rsem.at[8])

    def scale_gain(i, carry):
        wg_buf[pl.ds(pl.multiple_of(i * 112, 112), 112)] = (wg_recv[i].astype(F32) * gain_buf[...]).astype(BF)
        return carry

    lax.fori_loop(0, NX, scale_gain, 0)
    wait(att.at[pl.ds(0, NZ - 1)], rsem.at[4])

    proj = jnp.dot(wo_t[...], att[...].reshape(256, TOK), preferred_element_type=F32)
    rs1_send[...] = proj.astype(BF).reshape(32, 16, TOK)

    def rs1_hop(i, carry):
        xp, yp, cp = plane_peer(i)
        send(rs1_send.at[xp * 8 + yp * 2 + cp], rs1_recv.at[x * 8 + y * 2 + c], 5, dev(xp, yp, z, cp))
        return carry

    lax.fori_loop(1, 32, rs1_hop, 0)
    me = x * 8 + y * 2 + c
    rs1_recv[me] = rs1_send[me]

    @pl.when(x != y)
    def _():
        wait(res_recv, rsem.at[9])

    wait(rs1_recv.at[pl.ds(0, 31)], rsem.at[5])
    summed = jnp.sum(rs1_recv[...].astype(F32), axis=0)
    xt[z, y, c] = (res_recv[...].astype(F32) + summed).astype(BF)

    def s_hop(i, carry):
        send(xt.at[z, y, c], xt.at[z, y, c], 6, dev(x, y, zpeer(i), c))
        return carry

    lax.fori_loop(0, NZ - 1, s_hop, 0)

    @pl.when(x != y)
    def _():
        send(xt.at[z, y, c], str_recv, 12, dev(y, x, z, c))

    @pl.when(x == y)
    def _():
        str_recv[...] = xt[z, y, c]

    own_wd.wait()
    wait(wd_recv.at[pl.ds(0, NY - 1)], rsem.at[11])

    def down_block(i, carry):
        zero = jnp.zeros((HPAD - HID, 128), BF)
        tall = [
            jnp.concatenate([wd_recv[i, pl.ds(n * HID, HID)], zero], axis=0) for n in range(NZ)
        ]
        for n in range(NZ // 2):
            both = jnp.concatenate([tall[2 * n], tall[2 * n + 1]], axis=0)
            wd_t[pl.ds(pl.multiple_of(i * 128, 128), 128), pl.ds(n * 128, 128)] = both.T
        return carry

    lax.fori_loop(0, NY, down_block, 0)
    wait(xt.at[pl.ds(0, NZ - 1), 0, 0], rsem.at[6])

    def s2_hop(i, carry):
        yp, cp = (y + i // 2) % NY, (c + i % 2) % NC
        send(xt.at[:, y, c], xt.at[:, y, c], 7, dev(x, yp, z, cp))
        return carry

    lax.fori_loop(1, 8, s2_hop, 0)
    wait(xt.at[pl.ds(0, 14)], rsem.at[7])

    stream = xt[...].reshape(QD, TOK)
    wide = stream.astype(F32)
    squares = jnp.sum(wide * wide, axis=0, keepdims=True)
    part = jnp.dot(wg_buf[...], stream, preferred_element_type=F32)
    for i in range(NX):
        gsend[i, pl.ds(0, 112)] = part[i * 112 : (i + 1) * 112]
        gsend[i, pl.ds(112, 8)] = jnp.broadcast_to(squares, (8, TOK))

    def g_hop(d, carry):
        xp = (x + d) % NX
        send(gsend.at[xp], grecv.at[x], 13, dev(xp, y, z, c))
        return carry

    lax.fori_loop(1, NX, g_hop, 0)
    grecv[x] = gsend[x]
    wait(grecv.at[pl.ds(0, NX - 1)], rsem.at[13])
    gu = jnp.sum(grecv[...], axis=0)
    inv_rms = lax.rsqrt(gu[112:113] * (1.0 / (NX * QD)) + norm_eps)
    gate = gu[:HID] * inv_rms
    up = gu[HID : 2 * HID] * inv_rms
    hidden = gate / (1.0 + jnp.exp(-gate)) * up
    ht[z] = jnp.concatenate([hidden, jnp.zeros((HPAD - HID, TOK), F32)], axis=0).astype(BF)

    def h_hop(i, carry):
        send(ht.at[z], ht.at[z], 14, dev(x, y, zpeer(i), c))
        return carry

    lax.fori_loop(0, NZ - 1, h_hop, 0)
    wait(ht.at[pl.ds(0, NZ - 1)], rsem.at[14])

    down = jnp.dot(wd_t[...], ht[...].reshape(NZ * HPAD, TOK), preferred_element_type=F32)
    rs2_send[...] = down.astype(BF).reshape(32, 16, TOK)

    def rs2_hop(i, carry):
        xp, yp, cp = plane_peer(i)
        send(rs2_send.at[yp * 8 + xp * 2 + cp], rs2_recv.at[me], 15, dev(xp, yp, z, cp))
        return carry

    lax.fori_loop(1, 32, rs2_hop, 0)
    rs2_recv[me] = rs2_send[y * 8 + x * 2 + c]

    @pl.when(x != y)
    def _():
        wait(str_recv, rsem.at[12])

    wait(rs2_recv.at[pl.ds(0, 31)], rsem.at[15])
    result = str_recv[...].astype(F32) + jnp.sum(rs2_recv[...].astype(F32), axis=0)
    rounded = result.astype(BF)
    out_ref[0] = rounded[:, :64]
    out_ref[1] = rounded[:, 64:]

    wait(ysend.at[pl.ds(0, 3)], ssem.at[0])
    wait(ystat.at[pl.ds(0, 3)], ssem.at[1])
    wait(zsend.at[pl.ds(0, 15)], ssem.at[2])
    wait(zrstat.at[pl.ds(0, 15)], ssem.at[3])
    wait(att.at[pl.ds(0, 15)], ssem.at[4])
    wait(rs1_send.at[pl.ds(0, 31)], ssem.at[5])
    wait(xt.at[pl.ds(0, NZ - 1), 0, 0], ssem.at[6])
    wait(xt.at[pl.ds(0, 14)], ssem.at[7])
    wait(wg_recv.at[pl.ds(0, 3)], ssem.at[8])
    wait(wo_recv.at[pl.ds(0, 3)], ssem.at[10])
    wait(wd_recv.at[pl.ds(0, 3)], ssem.at[11])
    wait(gsend.at[pl.ds(0, 3)], ssem.at[13])
    wait(ht.at[pl.ds(0, 15)], ssem.at[14])
    wait(rs2_send.at[pl.ds(0, 31)], ssem.at[15])

    @pl.when(x != y)
    def _():
        wait(res_recv, ssem.at[9])
        wait(str_recv, ssem.at[12])


def body(
    resid,
    queries,
    new_kv,
    prefix_cache,
    suffix_cache,
    suffix_lengths,
    out_weight,
    norm_gain,
    gate_up,
    down_weight,
):
    seq_index = lax.axis_index("seq")
    requests, step_count, local_heads, head_dim = queries.shape
    prefix_len = prefix_cache.shape[1] * lax.axis_size("seq")
    cos_table, sin_table = rotary_tables(suffix_lengths, prefix_len, head_dim, step_count)
    rotated = rotate(queries, cos_table[:, :, None, :], sin_table[:, :, None, :])
    q_t = rotated.transpose(2, 3, 1, 0).reshape(local_heads, head_dim, TOK)
    own_cos = lax.dynamic_slice_in_dim(cos_table, seq_index, 1, 0)[0]
    own_sin = lax.dynamic_slice_in_dim(sin_table, seq_index, 1, 0)[0]
    new_keys = rotate(new_kv[0, 0, :, 0], own_cos, own_sin)
    fresh = jnp.stack([new_keys, new_kv[1, 0, :, 0]])
    fresh = jnp.pad(fresh, ((0, 0), (0, NEW - step_count), (0, 0)))
    resid_t = resid.transpose(2, 1, 0).reshape(128, TOK)
    wg = gate_up[:, :, 0, :].transpose(0, 2, 1).reshape(2 * HID, 4 * QD)
    any_spec = pl.BlockSpec(memory_space=pl.ANY)
    vmem = pltpu.VMEM
    result = pl.pallas_call(
        kernel,
        out_shape=jax.ShapeDtypeStruct((2, 16, 64), BF),
        in_specs=[pl.BlockSpec(memory_space=pltpu.SMEM)] + [any_spec] * 4
        + [pl.BlockSpec(memory_space=pltpu.VMEM)] + [any_spec] * 4,
        out_specs=pl.BlockSpec(memory_space=pltpu.VMEM),
        scratch_shapes=[
            vmem((HEADS, DH, TOK), BF), vmem((KEYS, DH), BF), vmem((KEYS, DH), BF), vmem((DH, KEYS), BF),
            vmem((NY, 256, TOK), BF), vmem((NY, 8, TOK), F32), vmem((NY, 256, TOK), BF), vmem((NY, 8, TOK), F32),
            vmem((NZ, 16, TOK), BF), vmem((2, 2, TOK), F32), vmem((NZ, 16, TOK), BF), vmem((NZ, 2, TOK), F32),
            vmem((NZ, 16, TOK), BF),
            vmem((NY, 256, 128), BF), vmem((512, 256), BF), vmem((32, 16, TOK), BF), vmem((32, 16, TOK), BF),
            vmem((16, TOK), BF),
            vmem((NZ, NY, NC, 16, TOK), BF), vmem((NX, 112, QD), BF), vmem((NX * 112, QD), BF), vmem((1, QD), F32),
            vmem((NX, 120, TOK), F32), vmem((NX, 120, TOK), F32),
            vmem((NZ, HPAD, TOK), BF), vmem((NY, 896, 128), BF), vmem((512, NZ * HPAD), BF),
            vmem((32, 16, TOK), BF), vmem((32, 16, TOK), BF), vmem((16, TOK), BF),
            pltpu.SemaphoreType.DMA((11,)), pltpu.SemaphoreType.DMA((16,)), pltpu.SemaphoreType.DMA((16,)),
        ],
        compiler_params=pltpu.CompilerParams(
            collective_id=0, has_side_effects=True, vmem_limit_bytes=40 * 1024 * 1024
        ),
        name="layer",
    )(
        suffix_lengths, q_t, fresh, prefix_cache[:, :, 0, :], suffix_cache[:, 0, :, 0, :], resid_t,
        out_weight, norm_gain.reshape(4, 1, QD), wg, down_weight,
    )
    return result.transpose(2, 0, 1)


def solution(mesh):
    placed = (
        P(None, None, "seq"),
        P(None, None, "kvh", None),
        P(None, "seq", None, "kvh", None),
        P(None, "seq", "kvh", None),
        P(None, "seq", None, "kvh", None),
        P(),
        P("kvh", "seq"),
        P(),
        P(None, None, "kvh", "seq"),
        P("kvh", "seq"),
    )
    return jax.shard_map(
        body, mesh=mesh, in_specs=placed, out_specs=P(None, None, ("seq", "kvh")), check_vma=False
    )
```

```python
import math

import jax
import jax.numpy as jnp
from jax import lax
from jax.experimental import pallas as pl
from jax.experimental.pallas import tpu as pltpu
from jax.sharding import PartitionSpec as P

theta_base = 500000.0
ntk_factor = 4.0
norm_eps = 1e-05
masked_score = -1e30

MESH = pl.DeviceIdType.MESH
NX, NY, NZ, NC = 4, 4, 16, 2
REQ = 64
TOK = 128
DH = 128
HEADS = 8
PRE, SUF, NEW = 512, 256, 128
KEYS = PRE + SUF + NEW
PREFIX = PRE * NY * NZ
ED = 1024
HID = 56
HPAD = 64
BF, F32 = jnp.bfloat16, jnp.float32
TN = (((0,), (0,)), ((), ()))


def rotary(position, index):
    growth = ntk_factor * (position + 1.0) / float(PREFIX // 4) - (ntk_factor - 1.0)
    log_base = math.log(theta_base) + DH / (DH - 2.0) * jnp.log(growth)
    angles = position * jnp.exp(log_base * (-2.0 * index.astype(F32) / DH))
    return jnp.cos(angles), jnp.sin(angles)


def dev(x, y, z, c):
    return (y * NZ + z, x * NC + c)


def kernel(
    lens_hbm, new_hbm, res_hbm, q_hbm, pre_hbm, suf_hbm, wo_hbm, gain_hbm, wg_hbm, wd_hbm,
    out_ref,
    lens_ref, new_ref, res_ref, q_raw, q_wide, q_buf, k_buf, v_buf, vt_buf, new_buf, res_t,
    ysend, ystat, yrecv, yrstat,
    zsend, zstat, zrecv, zrstat, att,
    wo_recv, wo_t, rs1_send, rs1_recv, res_recv,
    xt, wg_recv, wg_buf, gain_buf, gsend, grecv,
    ht, wd_recv, wd_t, rs2_send, rs2_recv, str_recv,
    loc, ssem, rsem,
):
    s = lax.axis_index("seq")
    k = lax.axis_index("kvh")
    x, c = k // NC, k % NC
    y, z = s // NZ, s % NZ
    zc, zi = z // 8, z % 8
    owner = c == zc

    def send(src, dst, stage, to):
        copy = pltpu.make_async_remote_copy(
            src_ref=src, dst_ref=dst, send_sem=ssem.at[stage], recv_sem=rsem.at[stage],
            device_id=to, device_id_type=MESH,
        )
        copy.start()

    def wait(ref, sem):
        pltpu.make_async_copy(ref, ref, sem).wait()

    def zpeer(i):
        return (z + 8 + ((i + 1) // 2) * (1 - 2 * (i % 2))) % NZ

    def plane_peer(i):
        return (x + i // 8) % NX, (y + (i // 2) % NY) % NY, (c + i % 2) % NC

    load_q = pltpu.make_async_copy(q_hbm, q_raw, loc.at[0])
    load_q.start()
    smalls = [
        pltpu.make_async_copy(lens_hbm, lens_ref, loc.at[9]),
        pltpu.make_async_copy(new_hbm, new_ref, loc.at[10]),
        pltpu.make_async_copy(res_hbm, res_ref, loc.at[11]),
    ]
    for copy in smalls:
        copy.start()
    loads = [
        pltpu.make_async_copy(pre_hbm.at[0], k_buf.at[pl.ds(0, PRE)], loc.at[1]),
        pltpu.make_async_copy(suf_hbm.at[0], k_buf.at[pl.ds(PRE, SUF)], loc.at[2]),
        pltpu.make_async_copy(pre_hbm.at[1], v_buf.at[pl.ds(0, PRE)], loc.at[3]),
        pltpu.make_async_copy(suf_hbm.at[1], v_buf.at[pl.ds(PRE, SUF)], loc.at[4]),
    ]
    for copy in loads:
        copy.start()

    barrier = pltpu.get_barrier_semaphore()

    def greet_z(i, carry):
        pl.semaphore_signal(barrier, inc=1, device_id=dev(x, y, zpeer(i), c), device_id_type=MESH)
        return carry

    def greet_plane(i, carry):
        xp, yp, cp = plane_peer(i)
        pl.semaphore_signal(barrier, inc=1, device_id=dev(xp, yp, z, cp), device_id_type=MESH)
        return carry

    lax.fori_loop(0, NZ - 1, greet_z, 0)
    lax.fori_loop(1, 32, greet_plane, 0)
    own_wg = pltpu.make_async_copy(wg_hbm.at[:, pl.ds(pl.multiple_of(k * ED, ED), ED)], wg_recv.at[k], loc.at[5])
    own_wo = pltpu.make_async_copy(wo_hbm.at[pl.ds(pl.multiple_of(y * 256, 256), 256)], wo_recv.at[y], loc.at[6])
    own_wd = pltpu.make_async_copy(wd_hbm.at[pl.ds(pl.multiple_of(y * 896, 896), 896)], wd_recv.at[y], loc.at[7])
    own_gain = pltpu.make_async_copy(gain_hbm.at[k], gain_buf, loc.at[8])
    for copy in (own_wg, own_wo, own_wd, own_gain):
        copy.start()

    for copy in smalls:
        copy.wait()
    lens = lens_ref[...]
    position = (PREFIX + jnp.concatenate([lens, lens + 1], axis=1)).astype(F32)
    cos, sin = rotary(position, lax.broadcasted_iota(jnp.int32, (DH // 2, TOK), 0))
    token = lax.broadcasted_iota(jnp.int32, (TOK, TOK), 0)
    place = lax.broadcasted_iota(jnp.int32, (TOK, TOK), 1)
    perm = (token == 2 * (place % REQ) + place // REQ).astype(F32).astype(BF)
    load_q.wait()
    q_wide[...] = q_raw[...].astype(F32).reshape(TOK * HEADS, DH)
    for h in range(HEADS):
        rows = q_wide[pl.ds(h, TOK, stride=HEADS)].astype(BF)
        turned = lax.dot_general(rows, perm, TN, preferred_element_type=F32)
        a, b = turned[: DH // 2], turned[DH // 2 :]
        q_buf[h // 2, :, pl.ds((h % 2) * TOK, TOK)] = jnp.concatenate(
            [a * cos - b * sin, b * cos + a * sin], axis=0
        ).astype(BF)

    own = lax.broadcasted_iota(jnp.int32, (1, REQ), 1) == s
    length = jnp.sum(jnp.where(own, lens.astype(F32), 0.0), axis=1, keepdims=True)
    lane8 = lax.broadcasted_iota(jnp.int32, (8, DH), 1)
    row8 = lax.broadcasted_iota(jnp.int32, (8, DH), 0)
    cos8, sin8 = rotary(PREFIX + length + row8.astype(F32), lane8 % (DH // 2))
    new_buf[...] = jnp.zeros_like(new_buf)
    new_buf[0, pl.ds(0, 2)] = new_ref[0].astype(F32)
    new_buf[1, pl.ds(0, 2)] = new_ref[1].astype(F32)
    fresh = new_buf[0]
    other = pltpu.roll(fresh, DH // 2, 1)
    fresh = fresh * cos8 + jnp.where(lane8 < DH // 2, -other, other) * sin8
    none = jnp.zeros((NEW - 8, DH), F32)
    k_buf[pl.ds(PRE + SUF, NEW)] = jnp.concatenate([fresh, none], axis=0).astype(BF)
    v_buf[pl.ds(PRE + SUF, NEW)] = jnp.concatenate([new_buf[1], none], axis=0).astype(BF)
    for copy in loads:
        copy.wait()
    vt_buf[...] = v_buf[...].T
    row = lax.broadcasted_iota(jnp.int32, (SUF + NEW, 2 * TOK), 0)
    lane = lax.broadcasted_iota(jnp.int32, (SUF + NEW, 2 * TOK), 1)
    live = (lane % REQ == s) & ((row.astype(F32) < length) | ((row >= SUF) & (row - SUF <= (lane // REQ) % 2)))
    scale = 1.0 / math.sqrt(DH)

    def attend(dst, stat, yq):
        raw = jnp.dot(k_buf[...], q_buf[yq], preferred_element_type=F32) * scale
        first = raw[:PRE]
        second = jnp.where(live, raw[PRE:], masked_score)
        peak = jnp.maximum(
            jnp.max(first, axis=0, keepdims=True), jnp.max(second, axis=0, keepdims=True)
        )
        e1 = jnp.exp(first - peak)
        e2 = jnp.exp(second - peak)
        total = jnp.sum(e1, axis=0, keepdims=True) + jnp.sum(e2, axis=0, keepdims=True)
        acc = jnp.dot(vt_buf[:, :PRE], e1.astype(BF), preferred_element_type=F32)
        acc = acc + jnp.dot(vt_buf[:, PRE:], e2.astype(BF), preferred_element_type=F32)
        for h in range(2):
            dst[pl.ds(h * DH, DH)] = acc[:, h * TOK : (h + 1) * TOK].astype(BF)
            stat[pl.ds(2 * h, 1)] = peak[:, h * TOK : (h + 1) * TOK]
            stat[pl.ds(2 * h + 1, 1)] = total[:, h * TOK : (h + 1) * TOK]

    def y_send(yp):
        send(ysend.at[yp], yrecv.at[y], 0, dev(x, yp, z, c))
        send(ystat.at[yp], yrstat.at[y], 1, dev(x, yp, z, c))

    first_y = (y + 2) % NY
    attend(ysend.at[first_y], ystat.at[first_y], first_y)
    pl.semaphore_wait(barrier, 46)
    y_send(first_y)

    def wg_hop(d, carry):
        kp = (k + d) % (NX * NC)
        send(wg_hbm.at[:, pl.ds(pl.multiple_of(kp * ED, ED), ED)], wg_recv.at[k], 8, dev(kp // NC, y, z, kp % NC))
        return carry

    lax.fori_loop(1, NX * NC, wg_hop, 0)

    def y_hop(d, carry):
        yp = (y + 2 * d - 1) % NY
        attend(ysend.at[yp], ystat.at[yp], yp)
        y_send(yp)
        return carry

    lax.fori_loop(1, 3, y_hop, 0)

    res_t[...] = lax.dot_general(res_ref[...], perm, TN, preferred_element_type=F32).astype(BF)

    @pl.when(owner & (x != y))
    def _():
        send(res_t.at[pl.ds(pl.multiple_of(x * 32, 32), 32)], res_recv, 9, dev(y, x, z, c))

    @pl.when(owner & (x == y))
    def _():
        res_recv[...] = res_t[pl.ds(pl.multiple_of(x * 32, 32), 32)]

    attend(yrecv.at[y], yrstat.at[y], y)
    wait(yrecv.at[pl.ds(0, NY - 1)], rsem.at[0])
    wait(yrstat.at[pl.ds(0, NY - 1)], rsem.at[1])

    for h in range(2):
        peaks = [yrstat[i, pl.ds(2 * h, 1)] for i in range(NY)]
        joint = jnp.maximum(jnp.maximum(peaks[0], peaks[1]), jnp.maximum(peaks[2], peaks[3]))
        facs = [jnp.exp(p - joint) for p in peaks]
        total = sum(yrstat[i, pl.ds(2 * h + 1, 1)] * facs[i] for i in range(NY))
        acc = sum(yrecv[i, pl.ds(h * DH, DH)].astype(F32) * facs[i] for i in range(NY))
        zsend[pl.ds(h * 8, 8)] = acc.astype(BF).reshape(8, 16, TOK)
        zstat[h, pl.ds(0, 1)] = joint
        zstat[h, pl.ds(1, 1)] = total

    def z_hop(i, carry):
        zp = zpeer(i)
        send(zstat.at[zp // 8], zrstat.at[z], 3, dev(x, y, zp, c))
        send(zsend.at[zp], zrecv.at[z], 2, dev(x, y, zp, c))
        return carry

    lax.fori_loop(0, NZ - 1, z_hop, 0)

    def wo_hop(d, carry):
        yp = (y + d) % NY
        send(wo_hbm.at[pl.ds(pl.multiple_of(yp * 256, 256), 256)], wo_recv.at[y], 10, dev(x, yp, z, c))
        return carry

    def wd_hop(d, carry):
        yp = (y + d) % NY
        send(wd_hbm.at[pl.ds(pl.multiple_of(yp * 896, 896), 896)], wd_recv.at[y], 11, dev(x, yp, z, c))
        return carry

    lax.fori_loop(1, NY, wo_hop, 0)
    lax.fori_loop(1, NY, wd_hop, 0)
    zrecv[z] = zsend[z]
    zrstat[z] = zstat[z // 8]
    wait(zrstat.at[pl.ds(0, NZ - 1)], rsem.at[3])
    wait(zrecv.at[pl.ds(0, NZ - 1)], rsem.at[2])

    peaks = [zrstat[i, pl.ds(0, 1)] for i in range(NZ)]
    joint = peaks[0]
    for p in peaks[1:]:
        joint = jnp.maximum(joint, p)
    facs = [jnp.exp(p - joint) for p in peaks]
    total = sum(zrstat[i, pl.ds(1, 1)] * facs[i] for i in range(NZ))
    acc = sum(zrecv[i].astype(F32) * facs[i] for i in range(NZ))
    att[z] = (acc / total).astype(BF)

    def a_hop(i, carry):
        send(att.at[z], att.at[z], 4, dev(x, y, zpeer(i), c))
        return carry

    lax.fori_loop(0, NZ - 1, a_hop, 0)

    own_wo.wait()
    wait(wo_recv.at[pl.ds(0, NY - 1)], rsem.at[10])
    for i in range(NY):
        wo_t[pl.ds(i * 128, 128)] = wo_recv[i].T
    wait(att.at[pl.ds(0, NZ - 1)], rsem.at[4])

    proj = jnp.dot(wo_t[...], att[...].reshape(256, TOK), preferred_element_type=F32)
    rs1_send[...] = proj.astype(BF).reshape(16, 32, TOK)
    me = x * 8 + y * 2 + c

    def rs1_hop(i, carry):
        xp, yp = (x + i // 4) % NX, (y + i % 4) % NY
        send(rs1_send.at[xp * 4 + yp], rs1_recv.at[me], 5, dev(xp, yp, z, zc))
        return carry

    lax.fori_loop(1, 16, rs1_hop, 0)

    @pl.when(jnp.logical_not(owner))
    def _():
        send(rs1_send.at[x * 4 + y], rs1_recv.at[me], 5, dev(x, y, z, zc))

    @pl.when(owner & (x != y))
    def _():
        wait(res_recv, rsem.at[9])

    @pl.when(owner)
    def _():
        rs1_recv[me] = rs1_send[x * 4 + y]
        wait(rs1_recv.at[pl.ds(0, 31)], rsem.at[5])
        summed = jnp.sum(rs1_recv[...].astype(F32), axis=0)
        xt[zi, y] = (res_recv[...].astype(F32) + summed).astype(BF)

        def s_hop(i, carry):
            send(xt.at[zi, y], xt.at[zi, y], 6, dev(x, y, zpeer(i), c))
            return carry

        lax.fori_loop(0, NZ - 1, s_hop, 0)
        for cp in range(NC):
            chunk = xt.at[zi, y, pl.ds(cp * 16, 16)]

            @pl.when((x != y) | (c != cp))
            def _():
                send(chunk, str_recv, 12, dev(y, x, z, cp))

            @pl.when((x == y) & (c == cp))
            def _():
                str_recv[...] = chunk[...]

    own_wg.wait()
    own_gain.wait()
    wait(wg_recv.at[pl.ds(0, 7)], rsem.at[8])

    def scale_gain(i, carry):
        wg_buf[pl.ds(pl.multiple_of(i * 112, 112), 112)] = (wg_recv[i].astype(F32) * gain_buf[...]).astype(BF)
        return carry

    lax.fori_loop(0, NX * NC, scale_gain, 0)

    @pl.when(owner)
    def _():
        wait(xt.at[pl.ds(0, 7), 0], rsem.at[6])

    @pl.when(jnp.logical_not(owner))
    def _():
        wait(xt.at[pl.ds(0, 8), 0], rsem.at[6])


    def s2_hop(d, carry):
        send(xt.at[:, y], xt.at[:, y], 7, dev(x, (y + d) % NY, z, c))
        return carry

    lax.fori_loop(1, NY, s2_hop, 0)
    wait(xt.at[:, pl.ds(0, 3)], rsem.at[7])

    stream = xt[...].reshape(ED, TOK)
    part = jnp.dot(wg_buf[...], stream, preferred_element_type=F32)
    gsend[:, pl.ds(0, 112)] = part.astype(BF).reshape(8, 112, TOK)
    wide = stream.astype(F32)
    squares = jnp.sum(wide * wide, axis=0, keepdims=True)
    high = squares.astype(BF).astype(F32)
    row16 = lax.broadcasted_iota(jnp.int32, (16, TOK), 0)
    both = jnp.where(row16 == 0, high, jnp.where(row16 == 1, squares - high, 0.0)).astype(BF)
    for i in range(8):
        gsend[i, pl.ds(112, 16)] = both

    def g_hop(d, carry):
        kp = (k + d) % (NX * NC)
        send(gsend.at[kp], grecv.at[k], 13, dev(kp // NC, y, z, kp % NC))
        return carry

    lax.fori_loop(1, NX * NC, g_hop, 0)
    grecv[k] = gsend[k]

    own_wd.wait()
    wait(wd_recv.at[pl.ds(0, NY - 1)], rsem.at[11])

    def down_block(i, carry):
        zero = jnp.zeros((HPAD - HID, 128), BF)
        tall = [
            jnp.concatenate([wd_recv[i, pl.ds(n * HID, HID)], zero], axis=0) for n in range(NZ)
        ]
        for n in range(NZ // 2):
            pair = jnp.concatenate([tall[2 * n], tall[2 * n + 1]], axis=0)
            wd_t[pl.ds(pl.multiple_of(i * 128, 128), 128), pl.ds(n * 128, 128)] = pair.T
        return carry

    lax.fori_loop(0, NY, down_block, 0)
    wait(grecv.at[pl.ds(0, 7)], rsem.at[13])
    gu = jnp.sum(grecv[...].astype(F32), axis=0)
    inv_rms = lax.rsqrt((gu[112:113] + gu[113:114]) * (1.0 / (8 * ED)) + norm_eps)
    gate = gu[:HID] * inv_rms
    up = gu[HID : 2 * HID] * inv_rms
    hidden = gate / (1.0 + jnp.exp(-gate)) * up
    ht[z] = jnp.concatenate([hidden, jnp.zeros((HPAD - HID, TOK), F32)], axis=0).astype(BF)

    def zd(d):
        return (z + d + NZ) % NZ

    def h_send(block, d, stage):
        send(ht.at[block], ht.at[block], stage, dev(x, y, zd(d), c))

    h_send(z, 5, 16)
    h_send(z, -5, 17)
    h_send(z, 8, 14)
    h_send(z, 2, 18)
    h_send(z, -2, 19)
    h_send(z, 1, 14)
    h_send(z, -1, 14)
    wait(ht.at[0], rsem.at[18])
    h_send(zd(-2), 1, 14)
    wait(ht.at[0], rsem.at[19])
    h_send(zd(2), -1, 14)
    wait(ht.at[0], rsem.at[16])
    h_send(zd(-5), 2, 14)
    h_send(zd(-5), 1, 14)
    h_send(zd(-5), -1, 14)
    wait(ht.at[0], rsem.at[17])
    h_send(zd(5), -2, 14)
    h_send(zd(5), -1, 14)
    h_send(zd(5), 1, 14)
    wait(ht.at[pl.ds(0, 11)], rsem.at[14])

    down = jnp.dot(wd_t[...], ht[...].reshape(NZ * HPAD, TOK), preferred_element_type=F32)
    rs2_send[...] = down.astype(BF).reshape(32, 16, TOK)

    def rs2_hop(i, carry):
        xp, yp, cp = plane_peer(i)
        send(rs2_send.at[yp * 8 + xp * 2 + cp], rs2_recv.at[me], 15, dev(xp, yp, z, cp))
        return carry

    lax.fori_loop(1, 32, rs2_hop, 0)
    rs2_recv[me] = rs2_send[y * 8 + x * 2 + c]

    @pl.when((x != y) | jnp.logical_not(owner))
    def _():
        wait(str_recv, rsem.at[12])

    wait(rs2_recv.at[pl.ds(0, 31)], rsem.at[15])
    result = str_recv[...].astype(F32) + jnp.sum(rs2_recv[...].astype(F32), axis=0)
    rounded = result.astype(BF)
    out_ref[0] = rounded[:, :REQ]
    out_ref[1] = rounded[:, REQ:]

    wait(ysend.at[pl.ds(0, 3)], ssem.at[0])
    wait(ystat.at[pl.ds(0, 3)], ssem.at[1])
    wait(zsend.at[pl.ds(0, 15)], ssem.at[2])
    wait(zrstat.at[pl.ds(0, 15)], ssem.at[3])
    wait(att.at[pl.ds(0, 15)], ssem.at[4])
    wait(rs1_send.at[pl.ds(0, 15)], ssem.at[5])
    wait(xt.at[:, pl.ds(0, 3)], ssem.at[7])
    wait(wg_recv.at[pl.ds(0, 7)], ssem.at[8])
    wait(wo_recv.at[pl.ds(0, 3)], ssem.at[10])
    wait(wd_recv.at[pl.ds(0, 3)], ssem.at[11])
    wait(gsend.at[pl.ds(0, 7)], ssem.at[13])
    wait(ht.at[pl.ds(0, 11)], ssem.at[14])
    wait(ht.at[0], ssem.at[16])
    wait(ht.at[0], ssem.at[17])
    wait(ht.at[0], ssem.at[18])
    wait(ht.at[0], ssem.at[19])
    wait(rs2_send.at[pl.ds(0, 31)], ssem.at[15])

    @pl.when(jnp.logical_not(owner))
    def _():
        wait(rs1_send.at[0], ssem.at[5])

    @pl.when(owner)
    def _():
        wait(xt.at[pl.ds(0, 5), pl.ds(0, 3)], ssem.at[6])

    @pl.when(owner & (x != y))
    def _():
        wait(res_recv, ssem.at[9])
        wait(res_recv, ssem.at[12])

    @pl.when(owner & (x == y))
    def _():
        wait(str_recv, ssem.at[12])


def body(
    resid,
    queries,
    new_kv,
    prefix_cache,
    suffix_cache,
    suffix_lengths,
    out_weight,
    norm_gain,
    gate_up,
    down_weight,
):
    hbm = pl.BlockSpec(memory_space=pl.ANY)
    vmem = pltpu.VMEM
    in_vmem = pl.BlockSpec(memory_space=vmem)
    result = pl.pallas_call(
        kernel,
        out_shape=jax.ShapeDtypeStruct((2, 16, REQ), BF),
        in_specs=[hbm] * 10,
        out_specs=in_vmem,
        scratch_shapes=[
            vmem((1, REQ), jnp.int32), vmem((2, 2, DH), BF), vmem((TOK, 128), BF),
            vmem((TOK, HEADS, DH), BF), vmem((TOK * HEADS, DH), F32), vmem((NY, DH, 2 * TOK), BF),
            vmem((KEYS, DH), BF), vmem((KEYS, DH), BF), vmem((DH, KEYS), BF), vmem((2, 8, DH), F32),
            vmem((128, TOK), BF),
            vmem((NY, 256, TOK), BF), vmem((NY, 8, TOK), F32), vmem((NY, 256, TOK), BF), vmem((NY, 8, TOK), F32),
            vmem((NZ, 16, TOK), BF), vmem((2, 2, TOK), F32), vmem((NZ, 16, TOK), BF), vmem((NZ, 2, TOK), F32),
            vmem((NZ, 16, TOK), BF),
            vmem((NY, 256, 128), BF), vmem((512, 256), BF), vmem((16, 32, TOK), BF), vmem((32, 32, TOK), BF),
            vmem((32, TOK), BF),
            vmem((8, NY, 32, TOK), BF), vmem((8, 112, ED), BF), vmem((8 * 112, ED), BF), vmem((1, ED), F32),
            vmem((8, 128, TOK), BF), vmem((8, 128, TOK), BF),
            vmem((NZ, HPAD, TOK), BF), vmem((NY, 896, 128), BF), vmem((512, NZ * HPAD), BF),
            vmem((32, 16, TOK), BF), vmem((32, 16, TOK), BF), vmem((16, TOK), BF),
            pltpu.SemaphoreType.DMA((12,)), pltpu.SemaphoreType.DMA((20,)), pltpu.SemaphoreType.DMA((20,)),
        ],
        compiler_params=pltpu.CompilerParams(
            collective_id=0, has_side_effects=True, vmem_limit_bytes=63 * 1024 * 1024
        ),
        name="layer",
    )(
        suffix_lengths.reshape(1, REQ), new_kv[:, 0, :, 0, :], resid.reshape(TOK, 128),
        queries.reshape(TOK, HEADS, DH), prefix_cache[:, :, 0, :], suffix_cache[:, 0, :, 0, :],
        out_weight, norm_gain.reshape(8, 1, ED), gate_up[:, :, 0, :].transpose(0, 2, 1).reshape(2 * HID, 8 * ED),
        down_weight,
    )
    return result.transpose(2, 0, 1)


def solution(mesh):
    placed = (
        P(None, None, "seq"),
        P(None, None, "kvh", None),
        P(None, "seq", None, "kvh", None),
        P(None, "seq", "kvh", None),
        P(None, "seq", None, "kvh", None),
        P(),
        P("kvh", "seq"),
        P(),
        P(None, None, "kvh", "seq"),
        P("kvh", "seq"),
    )
    return jax.shard_map(
        body, mesh=mesh, in_specs=placed, out_specs=P(None, None, ("seq", "kvh")), check_vma=False
    )
```

```python
import math

import jax
import jax.numpy as jnp
from jax import lax
from jax.experimental import pallas as pl
from jax.experimental.pallas import tpu as pltpu
from jax.sharding import PartitionSpec as P

theta_base = 500000.0
ntk_factor = 4.0
norm_eps = 1e-05
masked_score = -1e30

MESH = pl.DeviceIdType.MESH
NX, NY, NZ, NC = 4, 4, 16, 2
REQ = 64
TOK = 128
DH = 128
HEADS = 8
PRE, SUF, NEW = 512, 256, 128
KEYS = PRE + SUF + NEW
PREFIX = PRE * NY * NZ
ED = 1024
HID = 56
HPAD = 64
SX = 22
BF, F32 = jnp.bfloat16, jnp.float32
TN = (((0,), (0,)), ((), ()))


def rotary(position, index):
    growth = ntk_factor * (position + 1.0) / float(PREFIX // 4) - (ntk_factor - 1.0)
    log_base = math.log(theta_base) + DH / (DH - 2.0) * jnp.log(growth)
    angles = position * jnp.exp(log_base * (-2.0 * index.astype(F32) / DH))
    return jnp.cos(angles), jnp.sin(angles)


def dev(x, y, z, c):
    return (y * NZ + z, x * NC + c)


def kernel(
    lens_hbm, new_hbm, res_hbm, q_hbm, pre_hbm, suf_hbm, wo_hbm, gain_hbm, wg_hbm, wd_hbm,
    out_ref,
    lens_ref, new_ref, res_ref, q_raw, q_wide, q_buf, k_buf, v_buf, vt_buf, new_buf, res_t,
    ysend, ystat, yrecv, yrstat,
    zsend, zstat, lrecv, lstat, hrecv, hstat, att,
    wo_recv, wo_t, rs1_send, rs1_recv, res_recv,
    xt, wg_recv, wg_buf, gain_buf, gsend, grecv,
    ht, wd_recv, wd_t, rs2_send, rs2_recv, str_recv,
    loc, ssem, rsem,
):
    s = lax.axis_index("seq")
    k = lax.axis_index("kvh")
    x, c = k // NC, k % NC
    y, z = s // NZ, s % NZ
    zl, zh = z % 4, z // 4
    zc, zi = z // 8, z % 8
    owner = c == zc

    def send(src, dst, stage, to, at=None):
        at = stage if at is None else at
        copy = pltpu.make_async_remote_copy(
            src_ref=src, dst_ref=dst, send_sem=ssem.at[stage], recv_sem=rsem.at[at],
            device_id=to, device_id_type=MESH,
        )
        copy.start()

    def wait(ref, sem):
        pltpu.make_async_copy(ref, ref, sem).wait()

    xs = [x] + [lax.rem(x + d, NX) for d in range(1, NX)]
    ys = [y] + [lax.rem(y + d, NY) for d in range(1, NY)]
    zs = [z] + [lax.rem(z + d, NZ) for d in range(1, NZ)]
    cs = [c, 1 - c]
    z_order = sorted(range(1, NZ), key=lambda d: -min(d, NZ - d))
    zpeers = [(zs[d], dev(x, y, zs[d], c)) for d in z_order]
    near = [(d, (zh * 4 + lax.rem(zl + d, 4))) for d in (2, 1, 3)]
    near = [(zp % 4, dev(x, y, zp, c)) for _, zp in near]
    far = [dev(x, y, lax.rem(zh + d, 4) * 4 + zl, c) for d in (2, 1, 3)]
    plane = sorted(
        [(i, j, l) for i in range(NX) for j in range(NY) for l in range(NC) if i + j + l],
        key=lambda d: -(min(d[0], NX - d[0]) + min(d[1], NY - d[1])),
    )

    load_q = pltpu.make_async_copy(q_hbm, q_raw, loc.at[0])
    load_q.start()
    smalls = [
        pltpu.make_async_copy(lens_hbm, lens_ref, loc.at[9]),
        pltpu.make_async_copy(new_hbm, new_ref, loc.at[10]),
        pltpu.make_async_copy(res_hbm, res_ref, loc.at[11]),
    ]
    for copy in smalls:
        copy.start()
    loads = [
        pltpu.make_async_copy(pre_hbm.at[0], k_buf.at[pl.ds(0, PRE)], loc.at[1]),
        pltpu.make_async_copy(suf_hbm.at[0], k_buf.at[pl.ds(PRE, SUF)], loc.at[2]),
        pltpu.make_async_copy(pre_hbm.at[1], v_buf.at[pl.ds(0, PRE)], loc.at[3]),
        pltpu.make_async_copy(suf_hbm.at[1], v_buf.at[pl.ds(PRE, SUF)], loc.at[4]),
    ]
    for copy in loads:
        copy.start()

    barrier = pltpu.get_barrier_semaphore()

    def greet(to):
        pl.semaphore_signal(barrier, inc=1, device_id=to, device_id_type=MESH)

    for _, to in zpeers:
        greet(to)
    for i, j, l in plane:
        greet(dev(xs[i], ys[j], z, cs[l]))
    own_wg = pltpu.make_async_copy(wg_hbm.at[:, pl.ds(pl.multiple_of(k * ED, ED), ED)], wg_recv.at[k], loc.at[5])
    own_wo = pltpu.make_async_copy(wo_hbm.at[pl.ds(pl.multiple_of(y * 256, 256), 256)], wo_recv.at[y], loc.at[6])
    own_wd = pltpu.make_async_copy(wd_hbm.at[pl.ds(pl.multiple_of(y * 896, 896), 896)], wd_recv.at[y], loc.at[7])
    own_gain = pltpu.make_async_copy(gain_hbm.at[k], gain_buf, loc.at[8])
    for copy in (own_wg, own_wo, own_wd, own_gain):
        copy.start()

    for copy in smalls:
        copy.wait()
    lens = lens_ref[...]
    position = (PREFIX + jnp.concatenate([lens, lens + 1], axis=1)).astype(F32)
    cos, sin = rotary(position, lax.broadcasted_iota(jnp.int32, (DH // 2, TOK), 0))
    token = lax.broadcasted_iota(jnp.int32, (TOK, TOK), 0)
    place = lax.broadcasted_iota(jnp.int32, (TOK, TOK), 1)
    perm = (token == 2 * (place % REQ) + place // REQ).astype(F32).astype(BF)
    load_q.wait()
    q_wide[...] = q_raw[...].astype(F32).reshape(TOK * HEADS, DH)
    for h in range(HEADS):
        rows = q_wide[pl.ds(h, TOK, stride=HEADS)].astype(BF)
        turned = lax.dot_general(rows, perm, TN, preferred_element_type=F32)
        a, b = turned[: DH // 2], turned[DH // 2 :]
        q_buf[h // 2, :, pl.ds((h % 2) * TOK, TOK)] = jnp.concatenate(
            [a * cos - b * sin, b * cos + a * sin], axis=0
        ).astype(BF)

    own = lax.broadcasted_iota(jnp.int32, (1, REQ), 1) == s
    length = jnp.sum(jnp.where(own, lens.astype(F32), 0.0), axis=1, keepdims=True)
    lane8 = lax.broadcasted_iota(jnp.int32, (8, DH), 1)
    row8 = lax.broadcasted_iota(jnp.int32, (8, DH), 0)
    cos8, sin8 = rotary(PREFIX + length + row8.astype(F32), lane8 % (DH // 2))
    new_buf[...] = jnp.zeros_like(new_buf)
    new_buf[0, pl.ds(0, 2)] = new_ref[0].astype(F32)
    new_buf[1, pl.ds(0, 2)] = new_ref[1].astype(F32)
    fresh = new_buf[0]
    other = pltpu.roll(fresh, DH // 2, 1)
    fresh = fresh * cos8 + jnp.where(lane8 < DH // 2, -other, other) * sin8
    none = jnp.zeros((NEW - 8, DH), F32)
    k_buf[pl.ds(PRE + SUF, NEW)] = jnp.concatenate([fresh, none], axis=0).astype(BF)
    v_buf[pl.ds(PRE + SUF, NEW)] = jnp.concatenate([new_buf[1], none], axis=0).astype(BF)
    for copy in loads:
        copy.wait()
    vt_buf[...] = v_buf[...].T
    row = lax.broadcasted_iota(jnp.int32, (SUF + NEW, 2 * TOK), 0)
    lane = lax.broadcasted_iota(jnp.int32, (SUF + NEW, 2 * TOK), 1)
    live = (lane % REQ == s) & ((row.astype(F32) < length) | ((row >= SUF) & (row - SUF <= (lane // REQ) % 2)))
    scale = 1.0 / math.sqrt(DH)

    def attend(dst, stat, yq):
        raw = jnp.dot(k_buf[...], q_buf[yq], preferred_element_type=F32) * scale
        first = raw[:PRE]
        second = jnp.where(live, raw[PRE:], masked_score)
        peak = jnp.maximum(
            jnp.max(first, axis=0, keepdims=True), jnp.max(second, axis=0, keepdims=True)
        )
        e1 = jnp.exp(first - peak)
        e2 = jnp.exp(second - peak)
        total = jnp.sum(e1, axis=0, keepdims=True) + jnp.sum(e2, axis=0, keepdims=True)
        acc = jnp.dot(vt_buf[:, :PRE], e1.astype(BF), preferred_element_type=F32)
        acc = acc + jnp.dot(vt_buf[:, PRE:], e2.astype(BF), preferred_element_type=F32)
        for h in range(2):
            dst[pl.ds(h * DH, DH)] = acc[:, h * TOK : (h + 1) * TOK].astype(BF)
            stat[pl.ds(2 * h, 1)] = peak[:, h * TOK : (h + 1) * TOK]
            stat[pl.ds(2 * h + 1, 1)] = total[:, h * TOK : (h + 1) * TOK]

    def y_send(yp):
        send(ysend.at[yp], yrecv.at[y], 0, dev(x, yp, z, c))
        send(ystat.at[yp], yrstat.at[y], 1, dev(x, yp, z, c))

    for d in (2, 1, 3):
        attend(ysend.at[ys[d]], ystat.at[ys[d]], ys[d])
    pl.semaphore_wait(barrier, 46)
    for d in (2, 1, 3):
        y_send(ys[d])

    for i in (2, 1, 3):
        for l in range(NC):
            kp = xs[i] * NC + cs[l]
            send(wg_hbm.at[:, pl.ds(pl.multiple_of(kp * ED, ED), ED)], wg_recv.at[k], 8, dev(xs[i], y, z, cs[l]))
    send(
        wg_hbm.at[:, pl.ds(pl.multiple_of((x * NC + cs[1]) * ED, ED), ED)], wg_recv.at[k], 8, dev(x, y, z, cs[1])
    )

    res_t[...] = lax.dot_general(res_ref[...], perm, TN, preferred_element_type=F32).astype(BF)

    @pl.when(owner & (x != y))
    def _():
        send(res_t.at[pl.ds(pl.multiple_of(x * 32, 32), 32)], res_recv, 9, dev(y, x, z, c))

    @pl.when(owner & (x == y))
    def _():
        res_recv[...] = res_t[pl.ds(pl.multiple_of(x * 32, 32), 32)]

    attend(yrecv.at[y], yrstat.at[y], y)
    wait(yrecv.at[pl.ds(0, NY - 1)], rsem.at[0])
    wait(yrstat.at[pl.ds(0, NY - 1)], rsem.at[1])

    for h in range(2):
        peaks = [yrstat[i, pl.ds(2 * h, 1)] for i in range(NY)]
        joint = jnp.maximum(jnp.maximum(peaks[0], peaks[1]), jnp.maximum(peaks[2], peaks[3]))
        facs = [jnp.exp(p - joint) for p in peaks]
        total = sum(yrstat[i, pl.ds(2 * h + 1, 1)] * facs[i] for i in range(NY))
        acc = sum(yrecv[i, pl.ds(h * DH, DH)].astype(F32) * facs[i] for i in range(NY))
        zsend[pl.ds(h * 2, 2)] = acc.astype(BF).reshape(2, 64, TOK)
        zstat[h, pl.ds(0, 1)] = joint
        zstat[h, pl.ds(1, 1)] = total

    for zp, to in near:
        send(zsend.at[zp], lrecv.at[zl], 2, to)
        send(zstat.at[zp // 2], lstat.at[zl], 3, to)

    for d in (2, 1, 3):
        send(
            wo_hbm.at[pl.ds(pl.multiple_of(ys[d] * 256, 256), 256)], wo_recv.at[y], 10, dev(x, ys[d], z, c)
        )
    for d in (2, 1, 3):
        send(
            wd_hbm.at[pl.ds(pl.multiple_of(ys[d] * 896, 896), 896)], wd_recv.at[y], 11, dev(x, ys[d], z, c)
        )
    lrecv[zl] = zsend[zl]
    lstat[zl] = zstat[zl // 2]
    wait(lstat.at[pl.ds(0, 3)], rsem.at[3])
    wait(lrecv.at[pl.ds(0, 3)], rsem.at[2])

    def joined(parts, stats):
        peaks = [stats[i, pl.ds(0, 1)] for i in range(4)]
        joint = jnp.maximum(jnp.maximum(peaks[0], peaks[1]), jnp.maximum(peaks[2], peaks[3]))
        facs = [jnp.exp(p - joint) for p in peaks]
        total = sum(stats[i, pl.ds(1, 1)] * facs[i] for i in range(4))
        return joint, total, sum(parts[i].astype(F32) * facs[i] for i in range(4))

    joint, total, acc = joined(lrecv, lstat)
    hrecv[zh] = acc.astype(BF)
    hstat[zh, pl.ds(0, 1)] = joint
    hstat[zh, pl.ds(1, 1)] = total
    for to in far:
        send(hrecv.at[zh], hrecv.at[zh], 20, to)
        send(hstat.at[zh], hstat.at[zh], 21, to)
    wait(hstat.at[pl.ds(0, 3)], rsem.at[21])
    wait(hrecv.at[pl.ds(0, 3)], rsem.at[20])
    joint, total, acc = joined(hrecv, hstat)
    att[zl] = (acc / total).astype(BF)
    for _, to in near:
        send(att.at[zl], att.at[zl], 4, to)

    own_wo.wait()
    wait(wo_recv.at[pl.ds(0, NY - 1)], rsem.at[10])
    for i in range(NY):
        wo_t[pl.ds(i * 128, 128)] = wo_recv[i].T
    wait(att.at[pl.ds(0, 3)], rsem.at[4])

    proj = jnp.dot(wo_t[...], att[...].reshape(256, TOK), preferred_element_type=F32)
    rs1_send[...] = proj.astype(BF).reshape(16, 32, TOK)
    me = x * 8 + y * 2 + c

    for i, j, l in plane:
        if l == 0:
            send(rs1_send.at[xs[i] * 4 + ys[j]], rs1_recv.at[me], 5, dev(xs[i], ys[j], z, zc))

    @pl.when(jnp.logical_not(owner))
    def _():
        send(rs1_send.at[x * 4 + y], rs1_recv.at[me], 5, dev(x, y, z, zc))

    @pl.when(owner & (x != y))
    def _():
        wait(res_recv, rsem.at[9])

    @pl.when(owner)
    def _():
        rs1_recv[me] = rs1_send[x * 4 + y]
        wait(rs1_recv.at[pl.ds(0, 31)], rsem.at[5])
        summed = jnp.sum(rs1_recv[...].astype(F32), axis=0)
        xt[zi, y] = (res_recv[...].astype(F32) + summed).astype(BF)

        for _, to in zpeers:
            send(xt.at[zi, y], xt.at[zi, y], 6, to, SX + zi)
        for d in (2, 1, 3):
            send(xt.at[zi, y], xt.at[zi, y], 7, dev(x, ys[d], z, c))
        for cp in range(NC):
            chunk = xt.at[zi, y, pl.ds(cp * 16, 16)]

            @pl.when((x != y) | (c != cp))
            def _():
                send(chunk, str_recv, 12, dev(y, x, z, cp))

            @pl.when((x == y) & (c == cp))
            def _():
                str_recv[...] = chunk[...]

    up = (owner & (zi < 4)) | (jnp.logical_not(owner) & (zi >= 4))
    for j in range(8):
        i = jnp.where(up, j, 7 - j)

        @pl.when(jnp.logical_not(owner) | (i != zi))
        def _():
            wait(xt.at[i, y], rsem.at[SX + i])
            for d in (2, 1, 3):
                send(xt.at[i, y], xt.at[i, y], 7, dev(x, ys[d], z, c))

    own_wg.wait()
    own_gain.wait()
    wait(wg_recv.at[pl.ds(0, 7)], rsem.at[8])

    def scale_gain(i, carry):
        wg_buf[pl.ds(pl.multiple_of(i * 112, 112), 112)] = (wg_recv[i].astype(F32) * gain_buf[...]).astype(BF)
        return carry

    lax.fori_loop(0, NX * NC, scale_gain, 0)

    wait(xt.at[:, pl.ds(0, 3)], rsem.at[7])

    stream = xt[...].reshape(ED, TOK)
    part = jnp.dot(wg_buf[...], stream, preferred_element_type=F32)
    gsend[:, pl.ds(0, 112)] = part.astype(BF).reshape(8, 112, TOK)
    wide = stream.astype(F32)
    squares = jnp.sum(wide * wide, axis=0, keepdims=True)
    high = squares.astype(BF).astype(F32)
    row16 = lax.broadcasted_iota(jnp.int32, (16, TOK), 0)
    both = jnp.where(row16 == 0, high, jnp.where(row16 == 1, squares - high, 0.0)).astype(BF)
    for i in range(8):
        gsend[i, pl.ds(112, 16)] = both

    for i in (2, 1, 3, 0):
        for l in range(NC):
            if i + l:
                send(gsend.at[xs[i] * NC + cs[l]], grecv.at[k], 13, dev(xs[i], y, z, cs[l]))
    grecv[k] = gsend[k]

    own_wd.wait()
    wait(wd_recv.at[pl.ds(0, NY - 1)], rsem.at[11])

    def down_block(i, carry):
        zero = jnp.zeros((HPAD - HID, 128), BF)
        tall = [
            jnp.concatenate([wd_recv[i, pl.ds(n * HID, HID)], zero], axis=0) for n in range(NZ)
        ]
        for n in range(NZ // 2):
            pair = jnp.concatenate([tall[2 * n], tall[2 * n + 1]], axis=0)
            wd_t[pl.ds(pl.multiple_of(i * 128, 128), 128), pl.ds(n * 128, 128)] = pair.T
        return carry

    lax.fori_loop(0, NY, down_block, 0)

    wait(grecv.at[pl.ds(0, 7)], rsem.at[13])
    gu = jnp.sum(grecv[...].astype(F32), axis=0)
    inv_rms = lax.rsqrt((gu[112:113] + gu[113:114]) * (1.0 / (8 * ED)) + norm_eps)
    gate = gu[:HID] * inv_rms
    up = gu[HID : 2 * HID] * inv_rms
    hidden = gate / (1.0 + jnp.exp(-gate)) * up
    ht[z] = jnp.concatenate([hidden, jnp.zeros((HPAD - HID, TOK), F32)], axis=0).astype(BF)

    def zd(d):
        return zs[d % NZ]

    def h_send(block, d, stage):
        send(ht.at[block], ht.at[block], stage, dev(x, y, zd(d), c))

    h_send(z, 8, 14)
    h_send(z, 5, 16)
    h_send(z, -5, 17)
    h_send(z, 7, 14)
    h_send(z, -7, 14)
    h_send(z, 2, 18)
    h_send(z, -2, 19)
    h_send(z, 1, 14)
    h_send(z, -1, 14)
    wait(ht.at[0], rsem.at[18])
    h_send(zd(-2), 1, 14)
    wait(ht.at[0], rsem.at[19])
    h_send(zd(2), -1, 14)
    wait(ht.at[0], rsem.at[16])
    h_send(zd(-5), 1, 14)
    h_send(zd(-5), -1, 14)
    wait(ht.at[0], rsem.at[17])
    h_send(zd(5), -1, 14)
    h_send(zd(5), 1, 14)
    wait(ht.at[pl.ds(0, 11)], rsem.at[14])

    down = jnp.dot(wd_t[...], ht[...].reshape(NZ * HPAD, TOK), preferred_element_type=F32)
    rs2_send[...] = down.astype(BF).reshape(32, 16, TOK)

    for i, j, l in plane:
        send(rs2_send.at[ys[j] * 8 + xs[i] * 2 + cs[l]], rs2_recv.at[me], 15, dev(xs[i], ys[j], z, cs[l]))
    rs2_recv[me] = rs2_send[y * 8 + x * 2 + c]

    @pl.when((x != y) | jnp.logical_not(owner))
    def _():
        wait(str_recv, rsem.at[12])

    wait(rs2_recv.at[pl.ds(0, 31)], rsem.at[15])
    result = str_recv[...].astype(F32) + jnp.sum(rs2_recv[...].astype(F32), axis=0)
    rounded = result.astype(BF)
    out_ref[0] = rounded[:, :REQ]
    out_ref[1] = rounded[:, REQ:]

    wait(ysend.at[pl.ds(0, 3)], ssem.at[0])
    wait(ystat.at[pl.ds(0, 3)], ssem.at[1])
    wait(zsend.at[pl.ds(0, 3)], ssem.at[2])
    wait(lstat.at[pl.ds(0, 3)], ssem.at[3])
    wait(att.at[pl.ds(0, 3)], ssem.at[4])
    wait(hrecv.at[pl.ds(0, 3)], ssem.at[20])
    wait(hstat.at[pl.ds(0, 3)], ssem.at[21])
    wait(rs1_send.at[pl.ds(0, 15)], ssem.at[5])
    wait(xt.at[:, pl.ds(0, 3)], ssem.at[7])
    wait(wg_recv.at[pl.ds(0, 7)], ssem.at[8])
    wait(wo_recv.at[pl.ds(0, 3)], ssem.at[10])
    wait(wd_recv.at[pl.ds(0, 3)], ssem.at[11])
    wait(gsend.at[pl.ds(0, 7)], ssem.at[13])
    wait(ht.at[pl.ds(0, 11)], ssem.at[14])
    wait(ht.at[0], ssem.at[16])
    wait(ht.at[0], ssem.at[17])
    wait(ht.at[0], ssem.at[18])
    wait(ht.at[0], ssem.at[19])
    wait(rs2_send.at[pl.ds(0, 31)], ssem.at[15])

    @pl.when(jnp.logical_not(owner))
    def _():
        wait(rs1_send.at[0], ssem.at[5])

    @pl.when(owner)
    def _():
        wait(xt.at[pl.ds(0, 5), pl.ds(0, 3)], ssem.at[6])

    @pl.when(owner & (x != y))
    def _():
        wait(res_recv, ssem.at[9])
        wait(res_recv, ssem.at[12])

    @pl.when(owner & (x == y))
    def _():
        wait(str_recv, ssem.at[12])


def body(
    resid,
    queries,
    new_kv,
    prefix_cache,
    suffix_cache,
    suffix_lengths,
    out_weight,
    norm_gain,
    gate_up,
    down_weight,
):
    hbm = pl.BlockSpec(memory_space=pl.ANY)
    vmem = pltpu.VMEM
    in_vmem = pl.BlockSpec(memory_space=vmem)
    result = pl.pallas_call(
        kernel,
        out_shape=jax.ShapeDtypeStruct((2, 16, REQ), BF),
        in_specs=[hbm] * 10,
        out_specs=in_vmem,
        scratch_shapes=[
            vmem((1, REQ), jnp.int32), vmem((2, 2, DH), BF), vmem((TOK, 128), BF),
            vmem((TOK, HEADS, DH), BF), vmem((TOK * HEADS, DH), F32), vmem((NY, DH, 2 * TOK), BF),
            vmem((KEYS, DH), BF), vmem((KEYS, DH), BF), vmem((DH, KEYS), BF), vmem((2, 8, DH), F32),
            vmem((128, TOK), BF),
            vmem((NY, 256, TOK), BF), vmem((NY, 8, TOK), F32), vmem((NY, 256, TOK), BF), vmem((NY, 8, TOK), F32),
            vmem((4, 64, TOK), BF), vmem((2, 2, TOK), F32), vmem((4, 64, TOK), BF), vmem((4, 2, TOK), F32),
            vmem((4, 64, TOK), BF), vmem((4, 2, TOK), F32), vmem((4, 64, TOK), BF),
            vmem((NY, 256, 128), BF), vmem((512, 256), BF), vmem((16, 32, TOK), BF), vmem((32, 32, TOK), BF),
            vmem((32, TOK), BF),
            vmem((8, NY, 32, TOK), BF), vmem((8, 112, ED), BF), vmem((8 * 112, ED), BF), vmem((1, ED), F32),
            vmem((8, 128, TOK), BF), vmem((8, 128, TOK), BF),
            vmem((NZ, HPAD, TOK), BF), vmem((NY, 896, 128), BF), vmem((512, NZ * HPAD), BF),
            vmem((32, 16, TOK), BF), vmem((32, 16, TOK), BF), vmem((16, TOK), BF),
            pltpu.SemaphoreType.DMA((12,)), pltpu.SemaphoreType.DMA((22,)), pltpu.SemaphoreType.DMA((SX + 8,)),
        ],
        compiler_params=pltpu.CompilerParams(
            collective_id=0, has_side_effects=True, vmem_limit_bytes=63 * 1024 * 1024
        ),
        name="layer",
    )(
        suffix_lengths.reshape(1, REQ), new_kv[:, 0, :, 0, :], resid.reshape(TOK, 128),
        queries.reshape(TOK, HEADS, DH), prefix_cache[:, :, 0, :], suffix_cache[:, 0, :, 0, :],
        out_weight, norm_gain.reshape(8, 1, ED), gate_up[:, :, 0, :].transpose(0, 2, 1).reshape(2 * HID, 8 * ED),
        down_weight,
    )
    return result.transpose(2, 0, 1)


def solution(mesh):
    placed = (
        P(None, None, "seq"),
        P(None, None, "kvh", None),
        P(None, "seq", None, "kvh", None),
        P(None, "seq", "kvh", None),
        P(None, "seq", None, "kvh", None),
        P(),
        P("kvh", "seq"),
        P(),
        P(None, None, "kvh", "seq"),
        P("kvh", "seq"),
    )
    return jax.shard_map(
        body, mesh=mesh, in_specs=placed, out_specs=P(None, None, ("seq", "kvh")), check_vma=False
    )
```

```python
import math

import jax
import jax.numpy as jnp
from jax import lax
from jax.experimental import pallas as pl
from jax.experimental.pallas import tpu as pltpu
from jax.sharding import PartitionSpec as P

theta_base = 500000.0
ntk_factor = 4.0
norm_eps = 1e-05
masked_score = -1e30

MESH = pl.DeviceIdType.MESH
NX, NY, NZ, NC = 4, 4, 16, 2
REQ = 64
TOK = 128
DH = 128
HEADS = 8
PRE, SUF, NEW = 512, 256, 128
KEYS = PRE + SUF + NEW
PREFIX = PRE * NY * NZ
ED = 1024
HID = 56
HPAD = 64
SX = 22
BF, F32 = jnp.bfloat16, jnp.float32
TN = (((0,), (0,)), ((), ()))


def rotary(position, index):
    growth = ntk_factor * (position + 1.0) / float(PREFIX // 4) - (ntk_factor - 1.0)
    log_base = math.log(theta_base) + DH / (DH - 2.0) * jnp.log(growth)
    angles = position * jnp.exp(log_base * (-2.0 * index.astype(F32) / DH))
    return jnp.cos(angles), jnp.sin(angles)


def dev(x, y, z, c):
    return (y * NZ + z, x * NC + c)


def kernel(
    lens_hbm, new_hbm, res_hbm, q_hbm, pre_hbm, suf_hbm, wo_hbm, gain_hbm, wg_hbm, wd_hbm,
    out_ref,
    lens_ref, new_ref, res_ref, q_raw, q_wide, q_buf, k_buf, v_buf, vt_buf, new_buf, res_t,
    ysend, ystat, yrecv, yrstat,
    zsend, zstat, zrecv, zrstat, att,
    wo_recv, wo_t, rs1_send, rs1_recv, res_recv,
    xt, wg_recv, wg_buf, gain_buf, gsend, grecv,
    ht, wd_recv, wd_t, rs2_send, rs2_recv, str_recv,
    loc, ssem, rsem,
):
    s = lax.axis_index("seq")
    k = lax.axis_index("kvh")
    x, c = k // NC, k % NC
    y, z = s // NZ, s % NZ
    zc, zi = z // 8, z % 8
    owner = c == zc

    def send(src, dst, stage, to, at=None):
        at = stage if at is None else at
        copy = pltpu.make_async_remote_copy(
            src_ref=src, dst_ref=dst, send_sem=ssem.at[stage], recv_sem=rsem.at[at],
            device_id=to, device_id_type=MESH,
        )
        copy.start()

    def wait(ref, sem):
        pltpu.make_async_copy(ref, ref, sem).wait()

    xs = [x] + [lax.rem(x + d, NX) for d in range(1, NX)]
    ys = [y] + [lax.rem(y + d, NY) for d in range(1, NY)]
    zs = [z] + [lax.rem(z + d, NZ) for d in range(1, NZ)]
    cs = [c, 1 - c]
    z_order = sorted(range(1, NZ), key=lambda d: -min(d, NZ - d))
    zpeers = [(zs[d], dev(x, y, zs[d], c)) for d in z_order]
    plane = sorted(
        [(i, j, l) for i in range(NX) for j in range(NY) for l in range(NC) if i + j + l],
        key=lambda d: -(min(d[0], NX - d[0]) + min(d[1], NY - d[1])),
    )

    barrier = pltpu.get_barrier_semaphore()

    def greet(to):
        pl.semaphore_signal(barrier, inc=1, device_id=to, device_id_type=MESH)

    for _, to in zpeers:
        greet(to)
    for i, j, l in plane:
        greet(dev(xs[i], ys[j], z, cs[l]))

    load_q = pltpu.make_async_copy(q_hbm, q_raw, loc.at[0])
    load_q.start()
    smalls = [
        pltpu.make_async_copy(lens_hbm, lens_ref, loc.at[9]),
        pltpu.make_async_copy(new_hbm, new_ref, loc.at[10]),
        pltpu.make_async_copy(res_hbm, res_ref, loc.at[11]),
    ]
    for copy in smalls:
        copy.start()
    loads = [
        pltpu.make_async_copy(pre_hbm.at[0], k_buf.at[pl.ds(0, PRE)], loc.at[1]),
        pltpu.make_async_copy(suf_hbm.at[0], k_buf.at[pl.ds(PRE, SUF)], loc.at[2]),
        pltpu.make_async_copy(pre_hbm.at[1], v_buf.at[pl.ds(0, PRE)], loc.at[3]),
        pltpu.make_async_copy(suf_hbm.at[1], v_buf.at[pl.ds(PRE, SUF)], loc.at[4]),
    ]
    for copy in loads:
        copy.start()

    own_wg = pltpu.make_async_copy(wg_hbm.at[:, pl.ds(pl.multiple_of(k * ED, ED), ED)], wg_recv.at[k], loc.at[5])
    own_wo = pltpu.make_async_copy(wo_hbm.at[pl.ds(pl.multiple_of(y * 256, 256), 256)], wo_recv.at[y], loc.at[6])
    own_wd = pltpu.make_async_copy(wd_hbm.at[pl.ds(pl.multiple_of(y * 896, 896), 896)], wd_recv.at[y], loc.at[7])
    own_gain = pltpu.make_async_copy(gain_hbm.at[k], gain_buf, loc.at[8])
    for copy in (own_wg, own_wo, own_wd, own_gain):
        copy.start()

    for copy in smalls:
        copy.wait()
    lens = lens_ref[...]
    position = (PREFIX + jnp.concatenate([lens, lens + 1], axis=1)).astype(F32)
    cos, sin = rotary(position, lax.broadcasted_iota(jnp.int32, (DH // 2, TOK), 0))
    token = lax.broadcasted_iota(jnp.int32, (TOK, TOK), 0)
    place = lax.broadcasted_iota(jnp.int32, (TOK, TOK), 1)
    perm = (token == 2 * (place % REQ) + place // REQ).astype(F32).astype(BF)
    load_q.wait()
    q_wide[...] = q_raw[...].astype(F32).reshape(TOK * HEADS, DH)
    for h in range(HEADS):
        rows = q_wide[pl.ds(h, TOK, stride=HEADS)].astype(BF)
        turned = lax.dot_general(rows, perm, TN, preferred_element_type=F32)
        a, b = turned[: DH // 2], turned[DH // 2 :]
        q_buf[h // 2, :, pl.ds((h % 2) * TOK, TOK)] = jnp.concatenate(
            [a * cos - b * sin, b * cos + a * sin], axis=0
        ).astype(BF)

    own = lax.broadcasted_iota(jnp.int32, (1, REQ), 1) == s
    length = jnp.sum(jnp.where(own, lens.astype(F32), 0.0), axis=1, keepdims=True)
    lane8 = lax.broadcasted_iota(jnp.int32, (8, DH), 1)
    row8 = lax.broadcasted_iota(jnp.int32, (8, DH), 0)
    cos8, sin8 = rotary(PREFIX + length + row8.astype(F32), lane8 % (DH // 2))
    new_buf[...] = jnp.zeros_like(new_buf)
    new_buf[0, pl.ds(0, 2)] = new_ref[0].astype(F32)
    new_buf[1, pl.ds(0, 2)] = new_ref[1].astype(F32)
    fresh = new_buf[0]
    other = pltpu.roll(fresh, DH // 2, 1)
    fresh = fresh * cos8 + jnp.where(lane8 < DH // 2, -other, other) * sin8
    none = jnp.zeros((NEW - 8, DH), F32)
    k_buf[pl.ds(PRE + SUF, NEW)] = jnp.concatenate([fresh, none], axis=0).astype(BF)
    v_buf[pl.ds(PRE + SUF, NEW)] = jnp.concatenate([new_buf[1], none], axis=0).astype(BF)
    for copy in loads:
        copy.wait()
    vt_buf[...] = v_buf[...].T
    row = lax.broadcasted_iota(jnp.int32, (SUF + NEW, 2 * TOK), 0)
    lane = lax.broadcasted_iota(jnp.int32, (SUF + NEW, 2 * TOK), 1)
    live = (lane % REQ == s) & ((row.astype(F32) < length) | ((row >= SUF) & (row - SUF <= (lane // REQ) % 2)))
    scale = 1.0 / math.sqrt(DH)

    def attend(dst, stat, yq):
        raw = jnp.dot(k_buf[...], q_buf[yq], preferred_element_type=F32) * scale
        first = raw[:PRE]
        second = jnp.where(live, raw[PRE:], masked_score)
        peak = jnp.maximum(
            jnp.max(first, axis=0, keepdims=True), jnp.max(second, axis=0, keepdims=True)
        )
        e1 = jnp.exp(first - peak)
        e2 = jnp.exp(second - peak)
        total = jnp.sum(e1, axis=0, keepdims=True) + jnp.sum(e2, axis=0, keepdims=True)
        acc = jnp.dot(vt_buf[:, :PRE], e1.astype(BF), preferred_element_type=F32)
        acc = acc + jnp.dot(vt_buf[:, PRE:], e2.astype(BF), preferred_element_type=F32)
        for h in range(2):
            dst[pl.ds(h * DH, DH)] = acc[:, h * TOK : (h + 1) * TOK].astype(BF)
            stat[pl.ds(2 * h, 1)] = peak[:, h * TOK : (h + 1) * TOK]
            stat[pl.ds(2 * h + 1, 1)] = total[:, h * TOK : (h + 1) * TOK]

    def y_send(yp):
        send(ysend.at[yp], yrecv.at[y], 0, dev(x, yp, z, c))
        send(ystat.at[yp], yrstat.at[y], 1, dev(x, yp, z, c))

    def attend_block(i, carry):
        yq = lax.rem(y + 1 + i, NY)
        attend(ysend.at[yq], ystat.at[yq], yq)
        return carry

    lax.fori_loop(0, NY - 1, attend_block, 0)
    pl.semaphore_wait(barrier, 46)
    for d in (2, 1, 3):
        y_send(ys[d])

    for i in (2, 1, 3):
        for l in range(NC):
            kp = xs[i] * NC + cs[l]
            send(wg_hbm.at[:, pl.ds(pl.multiple_of(kp * ED, ED), ED)], wg_recv.at[k], 8, dev(xs[i], y, z, cs[l]))
    send(
        wg_hbm.at[:, pl.ds(pl.multiple_of((x * NC + cs[1]) * ED, ED), ED)], wg_recv.at[k], 8, dev(x, y, z, cs[1])
    )

    res_t[...] = lax.dot_general(res_ref[...], perm, TN, preferred_element_type=F32).astype(BF)

    @pl.when(owner & (x != y))
    def _():
        send(res_t.at[pl.ds(pl.multiple_of(x * 32, 32), 32)], res_recv, 9, dev(y, x, z, c))

    @pl.when(owner & (x == y))
    def _():
        res_recv[...] = res_t[pl.ds(pl.multiple_of(x * 32, 32), 32)]

    attend(yrecv.at[y], yrstat.at[y], y)
    wait(yrecv.at[pl.ds(0, NY - 1)], rsem.at[0])
    wait(yrstat.at[pl.ds(0, NY - 1)], rsem.at[1])

    for h in range(2):
        peaks = [yrstat[i, pl.ds(2 * h, 1)] for i in range(NY)]
        joint = jnp.maximum(jnp.maximum(peaks[0], peaks[1]), jnp.maximum(peaks[2], peaks[3]))
        facs = [jnp.exp(p - joint) for p in peaks]
        total = sum(yrstat[i, pl.ds(2 * h + 1, 1)] * facs[i] for i in range(NY))
        acc = sum(yrecv[i, pl.ds(h * DH, DH)].astype(F32) * facs[i] for i in range(NY))
        zsend[pl.ds(h * 8, 8)] = (acc / total).astype(BF).reshape(8, 16, TOK)
        zstat[h] = joint + jnp.log(total)

    for zp, to in zpeers:
        send(zstat.at[zp // 8], zrstat.at[z], 3, to)
        send(zsend.at[zp], zrecv.at[z], 2, to)

    for d in (2, 1, 3):
        send(
            wo_hbm.at[pl.ds(pl.multiple_of(ys[d] * 256, 256), 256)], wo_recv.at[y], 10, dev(x, ys[d], z, c)
        )
    for d in (2, 1, 3):
        send(
            wd_hbm.at[pl.ds(pl.multiple_of(ys[d] * 896, 896), 896)], wd_recv.at[y], 11, dev(x, ys[d], z, c)
        )
    zrecv[z] = zsend[z]
    zrstat[z] = zstat[z // 8]
    wait(zrstat.at[pl.ds(0, NZ - 1)], rsem.at[3])
    wait(zrecv.at[pl.ds(0, NZ - 1)], rsem.at[2])

    logs = [zrstat[i] for i in range(NZ)]
    joint = logs[0]
    for p in logs[1:]:
        joint = jnp.maximum(joint, p)
    facs = [jnp.exp(p - joint) for p in logs]
    acc = sum(zrecv[i].astype(F32) * facs[i] for i in range(NZ))
    att[z] = (acc / sum(facs)).astype(BF)

    for _, to in zpeers:
        send(att.at[z], att.at[z], 4, to)

    own_wo.wait()
    wait(wo_recv.at[pl.ds(0, NY - 1)], rsem.at[10])
    for i in range(NY):
        wo_t[pl.ds(i * 128, 128)] = wo_recv[i].T
    wait(att.at[pl.ds(0, NZ - 1)], rsem.at[4])

    me = x * 8 + y * 2 + c
    spread = att[...].reshape(256, TOK)

    def project(i, carry):
        xp = lax.rem(x + 2 + i, NX)
        rows = pl.ds(pl.multiple_of(xp * 128, 128), 128)
        proj = jnp.dot(wo_t[rows], spread, preferred_element_type=F32)
        rs1_send[pl.ds(xp * 4, 4)] = proj.astype(BF).reshape(4, 32, TOK)
        for j in (2, 1, 3):
            send(rs1_send.at[xp * 4 + ys[j]], rs1_recv.at[me], 5, dev(xp, ys[j], z, zc))

        @pl.when((xp != x) | jnp.logical_not(owner))
        def _():
            send(rs1_send.at[xp * 4 + y], rs1_recv.at[me], 5, dev(xp, y, z, zc))

        return carry

    lax.fori_loop(0, NX, project, 0)

    @pl.when(owner & (x != y))
    def _():
        wait(res_recv, rsem.at[9])

    @pl.when(owner)
    def _():
        rs1_recv[me] = rs1_send[x * 4 + y]
        wait(rs1_recv.at[pl.ds(0, 31)], rsem.at[5])
        summed = jnp.sum(rs1_recv[...].astype(F32), axis=0)
        xt[zi, y] = (res_recv[...].astype(F32) + summed).astype(BF)

        for _, to in zpeers:
            send(xt.at[zi, y], xt.at[zi, y], 6, to, SX + zi)
        for d in (2, 1, 3):
            send(xt.at[zi, y], xt.at[zi, y], 7, dev(x, ys[d], z, c))
        for cp in range(NC):
            chunk = xt.at[zi, y, pl.ds(cp * 16, 16)]

            @pl.when((x != y) | (c != cp))
            def _():
                send(chunk, str_recv, 12, dev(y, x, z, cp))

            @pl.when((x == y) & (c == cp))
            def _():
                str_recv[...] = chunk[...]

    up = (owner & (zi < 4)) | (jnp.logical_not(owner) & (zi >= 4))
    for j in range(8):
        i = jnp.where(up, j, 7 - j)

        @pl.when(jnp.logical_not(owner) | (i != zi))
        def _():
            wait(xt.at[i, y], rsem.at[SX + i])
            for d in (2, 1, 3):
                send(xt.at[i, y], xt.at[i, y], 7, dev(x, ys[d], z, c))

    own_wg.wait()
    own_gain.wait()
    wait(wg_recv.at[pl.ds(0, 7)], rsem.at[8])

    def scale_gain(i, carry):
        wg_buf[pl.ds(pl.multiple_of(i * 112, 112), 112)] = (wg_recv[i].astype(F32) * gain_buf[...]).astype(BF)
        return carry

    lax.fori_loop(0, NX * NC, scale_gain, 0)

    wait(xt.at[:, pl.ds(0, 3)], rsem.at[7])

    stream = xt[...].reshape(ED, TOK)
    wide = stream.astype(F32)
    squares = jnp.sum(wide * wide, axis=0, keepdims=True)
    high = squares.astype(BF).astype(F32)
    row16 = lax.broadcasted_iota(jnp.int32, (16, TOK), 0)
    both = jnp.where(row16 == 0, high, jnp.where(row16 == 1, squares - high, 0.0)).astype(BF)
    def gate_up_block(i, carry):
        kp = lax.rem(k + 4 + i, NX * NC)
        part = jnp.dot(
            wg_buf[pl.ds(pl.multiple_of(kp * 112, 112), 112)], stream, preferred_element_type=F32
        )
        gsend[kp, pl.ds(0, 112)] = part.astype(BF)
        gsend[kp, pl.ds(112, 16)] = both

        @pl.when(kp != k)
        def _():
            send(gsend.at[kp], grecv.at[k], 13, dev(kp // NC, y, z, kp % NC))

        return carry

    lax.fori_loop(0, NX * NC, gate_up_block, 0)
    grecv[k] = gsend[k]

    own_wd.wait()
    wait(wd_recv.at[pl.ds(0, NY - 1)], rsem.at[11])

    def down_block(i, carry):
        zero = jnp.zeros((HPAD - HID, 128), BF)
        tall = [
            jnp.concatenate([wd_recv[i, pl.ds(n * HID, HID)], zero], axis=0) for n in range(NZ)
        ]
        for n in range(NZ // 2):
            pair = jnp.concatenate([tall[2 * n], tall[2 * n + 1]], axis=0)
            wd_t[pl.ds(pl.multiple_of(i * 128, 128), 128), pl.ds(n * 128, 128)] = pair.T
        return carry

    lax.fori_loop(0, NY, down_block, 0)

    wait(grecv.at[pl.ds(0, 7)], rsem.at[13])
    gu = jnp.sum(grecv[...].astype(F32), axis=0)
    inv_rms = lax.rsqrt((gu[112:113] + gu[113:114]) * (1.0 / (8 * ED)) + norm_eps)
    gate = gu[:HID] * inv_rms
    up = gu[HID : 2 * HID] * inv_rms
    hidden = gate / (1.0 + jnp.exp(-gate)) * up
    ht[z] = jnp.concatenate([hidden, jnp.zeros((HPAD - HID, TOK), F32)], axis=0).astype(BF)

    def zd(d):
        return zs[d % NZ]

    def h_send(block, d, stage):
        send(ht.at[block], ht.at[block], stage, dev(x, y, zd(d), c))

    h_send(z, 5, 16)
    h_send(z, -5, 17)
    h_send(z, 8, 14)
    h_send(z, 2, 18)
    h_send(z, -2, 19)
    h_send(z, 1, 14)
    h_send(z, -1, 14)
    wait(ht.at[0], rsem.at[18])
    h_send(zd(-2), 1, 14)
    wait(ht.at[0], rsem.at[19])
    h_send(zd(2), -1, 14)
    wait(ht.at[0], rsem.at[16])
    h_send(zd(-5), 2, 14)
    h_send(zd(-5), 1, 14)
    h_send(zd(-5), -1, 14)
    wait(ht.at[0], rsem.at[17])
    h_send(zd(5), -2, 14)
    h_send(zd(5), -1, 14)
    h_send(zd(5), 1, 14)
    wait(ht.at[pl.ds(0, 11)], rsem.at[14])

    gathered = ht[...].reshape(NZ * HPAD, TOK)

    def down_project(i, carry):
        yp = lax.rem(y + 2 + i, NY)
        down = jnp.dot(
            wd_t[pl.ds(pl.multiple_of(yp * 128, 128), 128)], gathered, preferred_element_type=F32
        )
        rs2_send[pl.ds(yp * 8, 8)] = down.astype(BF).reshape(8, 16, TOK)
        for i in (2, 1, 3):
            for l in range(NC):
                send(rs2_send.at[yp * 8 + xs[i] * 2 + cs[l]], rs2_recv.at[me], 15, dev(xs[i], yp, z, cs[l]))
        send(rs2_send.at[yp * 8 + x * 2 + cs[1]], rs2_recv.at[me], 15, dev(x, yp, z, cs[1]))

        @pl.when(yp != y)
        def _():
            send(rs2_send.at[yp * 8 + k], rs2_recv.at[me], 15, dev(x, yp, z, c))

        return carry

    lax.fori_loop(0, NY, down_project, 0)
    rs2_recv[me] = rs2_send[y * 8 + x * 2 + c]

    @pl.when((x != y) | jnp.logical_not(owner))
    def _():
        wait(str_recv, rsem.at[12])

    wait(rs2_recv.at[pl.ds(0, 31)], rsem.at[15])
    result = str_recv[...].astype(F32) + jnp.sum(rs2_recv[...].astype(F32), axis=0)
    rounded = result.astype(BF)
    out_ref[0] = rounded[:, :REQ]
    out_ref[1] = rounded[:, REQ:]

    wait(ysend.at[pl.ds(0, 3)], ssem.at[0])
    wait(ystat.at[pl.ds(0, 3)], ssem.at[1])
    wait(zsend.at[pl.ds(0, 15)], ssem.at[2])
    wait(zrstat.at[pl.ds(0, 15)], ssem.at[3])
    wait(att.at[pl.ds(0, 15)], ssem.at[4])
    wait(rs1_send.at[pl.ds(0, 15)], ssem.at[5])
    wait(xt.at[:, pl.ds(0, 3)], ssem.at[7])
    wait(wg_recv.at[pl.ds(0, 7)], ssem.at[8])
    wait(wo_recv.at[pl.ds(0, 3)], ssem.at[10])
    wait(wd_recv.at[pl.ds(0, 3)], ssem.at[11])
    wait(gsend.at[pl.ds(0, 7)], ssem.at[13])
    wait(ht.at[pl.ds(0, 11)], ssem.at[14])
    wait(ht.at[0], ssem.at[16])
    wait(ht.at[0], ssem.at[17])
    wait(ht.at[0], ssem.at[18])
    wait(ht.at[0], ssem.at[19])
    wait(rs2_send.at[pl.ds(0, 31)], ssem.at[15])

    @pl.when(jnp.logical_not(owner))
    def _():
        wait(rs1_send.at[0], ssem.at[5])

    @pl.when(owner)
    def _():
        wait(xt.at[pl.ds(0, 5), pl.ds(0, 3)], ssem.at[6])

    @pl.when(owner & (x != y))
    def _():
        wait(res_recv, ssem.at[9])
        wait(res_recv, ssem.at[12])

    @pl.when(owner & (x == y))
    def _():
        wait(str_recv, ssem.at[12])


def body(
    resid,
    queries,
    new_kv,
    prefix_cache,
    suffix_cache,
    suffix_lengths,
    out_weight,
    norm_gain,
    gate_up,
    down_weight,
):
    hbm = pl.BlockSpec(memory_space=pl.ANY)
    vmem = pltpu.VMEM
    in_vmem = pl.BlockSpec(memory_space=vmem)
    result = pl.pallas_call(
        kernel,
        out_shape=jax.ShapeDtypeStruct((2, 16, REQ), BF),
        in_specs=[hbm] * 10,
        out_specs=in_vmem,
        scratch_shapes=[
            vmem((1, REQ), jnp.int32), vmem((2, 2, DH), BF), vmem((TOK, 128), BF),
            vmem((TOK, HEADS, DH), BF), vmem((TOK * HEADS, DH), F32), vmem((NY, DH, 2 * TOK), BF),
            vmem((KEYS, DH), BF), vmem((KEYS, DH), BF), vmem((DH, KEYS), BF), vmem((2, 8, DH), F32),
            vmem((128, TOK), BF),
            vmem((NY, 256, TOK), BF), vmem((NY, 8, TOK), F32), vmem((NY, 256, TOK), BF), vmem((NY, 8, TOK), F32),
            vmem((NZ, 16, TOK), BF), vmem((2, 1, TOK), F32), vmem((NZ, 16, TOK), BF), vmem((NZ, 1, TOK), F32),
            vmem((NZ, 16, TOK), BF),
            vmem((NY, 256, 128), BF), vmem((512, 256), BF), vmem((16, 32, TOK), BF), vmem((32, 32, TOK), BF),
            vmem((32, TOK), BF),
            vmem((8, NY, 32, TOK), BF), vmem((8, 112, ED), BF), vmem((8 * 112, ED), BF), vmem((1, ED), F32),
            vmem((8, 128, TOK), BF), vmem((8, 128, TOK), BF),
            vmem((NZ, HPAD, TOK), BF), vmem((NY, 896, 128), BF), vmem((512, NZ * HPAD), BF),
            vmem((32, 16, TOK), BF), vmem((32, 16, TOK), BF), vmem((16, TOK), BF),
            pltpu.SemaphoreType.DMA((12,)), pltpu.SemaphoreType.DMA((22,)), pltpu.SemaphoreType.DMA((SX + 8,)),
        ],
        compiler_params=pltpu.CompilerParams(
            collective_id=0, has_side_effects=True, vmem_limit_bytes=63 * 1024 * 1024
        ),
        name="layer",
    )(
        suffix_lengths.reshape(1, REQ), new_kv[:, 0, :, 0, :], resid.reshape(TOK, 128),
        queries.reshape(TOK, HEADS, DH), prefix_cache[:, :, 0, :], suffix_cache[:, 0, :, 0, :],
        out_weight, norm_gain.reshape(8, 1, ED), gate_up[:, :, 0, :].transpose(0, 2, 1).reshape(2 * HID, 8 * ED),
        down_weight,
    )
    return result.transpose(2, 0, 1)


def solution(mesh):
    placed = (
        P(None, None, "seq"),
        P(None, None, "kvh", None),
        P(None, "seq", None, "kvh", None),
        P(None, "seq", "kvh", None),
        P(None, "seq", None, "kvh", None),
        P(),
        P("kvh", "seq"),
        P(),
        P(None, None, "kvh", "seq"),
        P("kvh", "seq"),
    )
    return jax.shard_map(
        body, mesh=mesh, in_specs=placed, out_specs=P(None, None, ("seq", "kvh")), check_vma=False
    )
```

```python
import math

import jax
import jax.numpy as jnp
from jax import lax
from jax.experimental import pallas as pl
from jax.experimental.pallas import tpu as pltpu
from jax.sharding import PartitionSpec as P

theta_base = 500000.0
ntk_factor = 4.0
norm_eps = 1e-05
masked_score = -1e30

MESH = pl.DeviceIdType.MESH
NX, NY, NZ, NC = 4, 4, 16, 2
REQ = 64
TOK = 128
DH = 128
HEADS = 8
PRE, SUF, NEW = 512, 256, 128
KEYS = PRE + SUF + NEW
PREFIX = PRE * NY * NZ
ED = 1024
HID = 56
HPAD = 64
SX = 22
BF, F32 = jnp.bfloat16, jnp.float32
TN = (((0,), (0,)), ((), ()))


def rotary(position, index):
    growth = ntk_factor * (position + 1.0) / float(PREFIX // 4) - (ntk_factor - 1.0)
    log_base = math.log(theta_base) + DH / (DH - 2.0) * jnp.log(growth)
    angles = position * jnp.exp(log_base * (-2.0 * index.astype(F32) / DH))
    return jnp.cos(angles), jnp.sin(angles)


def dev(x, y, z, c):
    return (y * NZ + z, x * NC + c)


def kernel(
    lens_hbm, new_hbm, res_hbm, q_hbm, pre_hbm, suf_hbm, wo_hbm, gain_hbm, wg_hbm, wd_hbm,
    out_ref,
    lens_ref, new_ref, res_ref, q_raw, q_wide, q_buf, k_buf, v_buf, vt_buf, new_buf, res_t,
    ysend, ystat, yrecv, yrstat,
    zsend, zstat, zrecv, zrstat, att,
    wo_recv, wo_t, rs1_send, rs1_recv, res_recv,
    xt, wg_recv, wg_buf, gain_buf, gsend, grecv,
    ht, wd_recv, wd_t, rs2_send, rs2_recv, str_recv,
    loc, ssem, rsem,
):
    s = lax.axis_index("seq")
    k = lax.axis_index("kvh")
    x, c = k // NC, k % NC
    y, z = s // NZ, s % NZ
    zc, zi = z // 8, z % 8
    owner = c == zc

    def send(src, dst, stage, to, at=None):
        at = stage if at is None else at
        copy = pltpu.make_async_remote_copy(
            src_ref=src, dst_ref=dst, send_sem=ssem.at[stage], recv_sem=rsem.at[at],
            device_id=to, device_id_type=MESH,
        )
        copy.start()

    def wait(ref, sem):
        pltpu.make_async_copy(ref, ref, sem).wait()

    xs = [x] + [lax.rem(x + d, NX) for d in range(1, NX)]
    ys = [y] + [lax.rem(y + d, NY) for d in range(1, NY)]
    zs = [z] + [lax.rem(z + d, NZ) for d in range(1, NZ)]
    cs = [c, 1 - c]
    z_order = sorted(range(1, NZ), key=lambda d: -min(d, NZ - d))
    zpeers = [(zs[d], dev(x, y, zs[d], c)) for d in z_order]
    plane = sorted(
        [(i, j, l) for i in range(NX) for j in range(NY) for l in range(NC) if i + j + l],
        key=lambda d: -(min(d[0], NX - d[0]) + min(d[1], NY - d[1])),
    )

    barrier = pltpu.get_barrier_semaphore()

    def greet(to):
        pl.semaphore_signal(barrier, inc=1, device_id=to, device_id_type=MESH)

    for _, to in zpeers:
        greet(to)
    for i, j, l in plane:
        greet(dev(xs[i], ys[j], z, cs[l]))

    load_q = pltpu.make_async_copy(q_hbm, q_raw, loc.at[0])
    load_q.start()
    smalls = [
        pltpu.make_async_copy(lens_hbm, lens_ref, loc.at[9]),
        pltpu.make_async_copy(new_hbm, new_ref, loc.at[10]),
        pltpu.make_async_copy(res_hbm, res_ref, loc.at[11]),
    ]
    for copy in smalls:
        copy.start()
    loads = [
        pltpu.make_async_copy(pre_hbm.at[0], k_buf.at[pl.ds(0, PRE)], loc.at[1]),
        pltpu.make_async_copy(suf_hbm.at[0], k_buf.at[pl.ds(PRE, SUF)], loc.at[2]),
        pltpu.make_async_copy(pre_hbm.at[1], v_buf.at[pl.ds(0, PRE)], loc.at[3]),
        pltpu.make_async_copy(suf_hbm.at[1], v_buf.at[pl.ds(PRE, SUF)], loc.at[4]),
    ]
    for copy in loads:
        copy.start()

    own_wg = pltpu.make_async_copy(wg_hbm.at[:, pl.ds(pl.multiple_of(k * ED, ED), ED)], wg_recv.at[k], loc.at[5])
    own_wo = pltpu.make_async_copy(wo_hbm.at[pl.ds(pl.multiple_of(y * 256, 256), 256)], wo_recv.at[y], loc.at[6])
    own_wd = pltpu.make_async_copy(wd_hbm.at[pl.ds(pl.multiple_of(y * 896, 896), 896)], wd_recv.at[y], loc.at[7])
    own_gain = pltpu.make_async_copy(gain_hbm.at[k], gain_buf, loc.at[8])
    for copy in (own_wg, own_wo, own_wd, own_gain):
        copy.start()

    for copy in smalls:
        copy.wait()
    lens = lens_ref[...]
    position = (PREFIX + jnp.concatenate([lens, lens + 1], axis=1)).astype(F32)
    cos, sin = rotary(position, lax.broadcasted_iota(jnp.int32, (DH // 2, TOK), 0))
    token = lax.broadcasted_iota(jnp.int32, (TOK, TOK), 0)
    place = lax.broadcasted_iota(jnp.int32, (TOK, TOK), 1)
    perm = (token == 2 * (place % REQ) + place // REQ).astype(F32).astype(BF)
    load_q.wait()
    q_wide[...] = q_raw[...].astype(F32).reshape(TOK * HEADS, DH)
    for h in range(HEADS):
        rows = q_wide[pl.ds(h, TOK, stride=HEADS)].astype(BF)
        turned = lax.dot_general(rows, perm, TN, preferred_element_type=F32)
        a, b = turned[: DH // 2], turned[DH // 2 :]
        q_buf[h // 2, :, pl.ds((h % 2) * TOK, TOK)] = jnp.concatenate(
            [a * cos - b * sin, b * cos + a * sin], axis=0
        ).astype(BF)

    own = lax.broadcasted_iota(jnp.int32, (1, REQ), 1) == s
    length = jnp.sum(jnp.where(own, lens.astype(F32), 0.0), axis=1, keepdims=True)
    lane8 = lax.broadcasted_iota(jnp.int32, (8, DH), 1)
    row8 = lax.broadcasted_iota(jnp.int32, (8, DH), 0)
    cos8, sin8 = rotary(PREFIX + length + row8.astype(F32), lane8 % (DH // 2))
    new_buf[...] = jnp.zeros_like(new_buf)
    new_buf[0, pl.ds(0, 2)] = new_ref[0].astype(F32)
    new_buf[1, pl.ds(0, 2)] = new_ref[1].astype(F32)
    fresh = new_buf[0]
    other = pltpu.roll(fresh, DH // 2, 1)
    fresh = fresh * cos8 + jnp.where(lane8 < DH // 2, -other, other) * sin8
    none = jnp.zeros((NEW - 8, DH), F32)
    k_buf[pl.ds(PRE + SUF, NEW)] = jnp.concatenate([fresh, none], axis=0).astype(BF)
    v_buf[pl.ds(PRE + SUF, NEW)] = jnp.concatenate([new_buf[1], none], axis=0).astype(BF)
    for copy in loads:
        copy.wait()
    vt_buf[...] = v_buf[...].T
    row = lax.broadcasted_iota(jnp.int32, (SUF + NEW, 2 * TOK), 0)
    lane = lax.broadcasted_iota(jnp.int32, (SUF + NEW, 2 * TOK), 1)
    live = (lane % REQ == s) & ((row.astype(F32) < length) | ((row >= SUF) & (row - SUF <= (lane // REQ) % 2)))
    scale = 1.0 / math.sqrt(DH)

    def attend(dst, stat, yq):
        raw = jnp.dot(k_buf[...], q_buf[yq], preferred_element_type=F32) * scale
        first = raw[:PRE]
        second = jnp.where(live, raw[PRE:], masked_score)
        peak = jnp.maximum(
            jnp.max(first, axis=0, keepdims=True), jnp.max(second, axis=0, keepdims=True)
        )
        e1 = jnp.exp(first - peak)
        e2 = jnp.exp(second - peak)
        total = jnp.sum(e1, axis=0, keepdims=True) + jnp.sum(e2, axis=0, keepdims=True)
        acc = jnp.dot(vt_buf[:, :PRE], e1.astype(BF), preferred_element_type=F32)
        acc = acc + jnp.dot(vt_buf[:, PRE:], e2.astype(BF), preferred_element_type=F32)
        for h in range(2):
            dst[pl.ds(h * DH, DH)] = acc[:, h * TOK : (h + 1) * TOK].astype(BF)
            stat[pl.ds(2 * h, 1)] = peak[:, h * TOK : (h + 1) * TOK]
            stat[pl.ds(2 * h + 1, 1)] = total[:, h * TOK : (h + 1) * TOK]

    def y_send(yp):
        send(ysend.at[yp], yrecv.at[y], 0, dev(x, yp, z, c))
        send(ystat.at[yp], yrstat.at[y], 1, dev(x, yp, z, c))

    def attend_block(i, carry):
        yq = lax.rem(y + 1 + i, NY)
        attend(ysend.at[yq], ystat.at[yq], yq)
        return carry

    lax.fori_loop(0, NY - 1, attend_block, 0)
    pl.semaphore_wait(barrier, 46)
    for d in (2, 1, 3):
        y_send(ys[d])

    for i in (2, 1, 3):
        for l in range(NC):
            kp = xs[i] * NC + cs[l]
            send(wg_hbm.at[:, pl.ds(pl.multiple_of(kp * ED, ED), ED)], wg_recv.at[k], 8, dev(xs[i], y, z, cs[l]))
    send(
        wg_hbm.at[:, pl.ds(pl.multiple_of((x * NC + cs[1]) * ED, ED), ED)], wg_recv.at[k], 8, dev(x, y, z, cs[1])
    )

    res_t[...] = lax.dot_general(res_ref[...], perm, TN, preferred_element_type=F32).astype(BF)

    @pl.when(owner & (x != y))
    def _():
        send(res_t.at[pl.ds(pl.multiple_of(x * 32, 32), 32)], res_recv, 9, dev(y, x, z, c))

    @pl.when(owner & (x == y))
    def _():
        res_recv[...] = res_t[pl.ds(pl.multiple_of(x * 32, 32), 32)]

    attend(yrecv.at[y], yrstat.at[y], y)
    wait(yrecv.at[pl.ds(0, NY - 1)], rsem.at[0])
    wait(yrstat.at[pl.ds(0, NY - 1)], rsem.at[1])

    for h in range(2):
        peaks = [yrstat[i, pl.ds(2 * h, 1)] for i in range(NY)]
        joint = jnp.maximum(jnp.maximum(peaks[0], peaks[1]), jnp.maximum(peaks[2], peaks[3]))
        facs = [jnp.exp(p - joint) for p in peaks]
        total = sum(yrstat[i, pl.ds(2 * h + 1, 1)] * facs[i] for i in range(NY))
        acc = sum(yrecv[i, pl.ds(h * DH, DH)].astype(F32) * facs[i] for i in range(NY))
        zsend[pl.ds(h * 8, 8)] = (acc / total).astype(BF).reshape(8, 16, TOK)
        zstat[h] = joint + jnp.log(total)

    for zp, to in zpeers:
        send(zstat.at[zp // 8], zrstat.at[z], 3, to)
        send(zsend.at[zp], zrecv.at[z], 2, to)

    for d in (2, 1, 3):
        send(
            wo_hbm.at[pl.ds(pl.multiple_of(ys[d] * 256, 256), 256)], wo_recv.at[y], 10, dev(x, ys[d], z, c)
        )
    for d in (2, 1, 3):
        send(
            wd_hbm.at[pl.ds(pl.multiple_of(ys[d] * 896, 896), 896)], wd_recv.at[y], 11, dev(x, ys[d], z, c)
        )
    zrecv[z] = zsend[z]
    zrstat[z] = zstat[z // 8]
    wait(zrstat.at[pl.ds(0, NZ - 1)], rsem.at[3])
    wait(zrecv.at[pl.ds(0, NZ - 1)], rsem.at[2])

    logs = zrstat[...].reshape(NZ, TOK)
    facs = jnp.exp(logs - jnp.max(logs, axis=0, keepdims=True))
    acc = jnp.sum(zrecv[...].astype(F32) * facs[:, None, :], axis=0)
    att[z] = (acc / jnp.sum(facs, axis=0, keepdims=True)).astype(BF)

    for _, to in zpeers:
        send(att.at[z], att.at[z], 4, to)

    own_wo.wait()
    wait(wo_recv.at[pl.ds(0, NY - 1)], rsem.at[10])
    for i in range(NY):
        wo_t[pl.ds(i * 128, 128)] = wo_recv[i].T
    wait(att.at[pl.ds(0, NZ - 1)], rsem.at[4])

    me = x * 8 + y * 2 + c
    spread = att[...].reshape(256, TOK)

    def project(i, carry):
        xp = xs[(2, 3, 1, 0)[i]]
        rows = pl.ds(pl.multiple_of(xp * 128, 128), 128)
        proj = jnp.dot(wo_t[rows], spread, preferred_element_type=F32)
        rs1_send[pl.ds(xp * 4, 4)] = proj.astype(BF).reshape(4, 32, TOK)
        for j in (2, 1, 3):
            send(rs1_send.at[xp * 4 + ys[j]], rs1_recv.at[me], 5, dev(xp, ys[j], z, zc))

        @pl.when((xp != x) | jnp.logical_not(owner))
        def _():
            send(rs1_send.at[xp * 4 + y], rs1_recv.at[me], 5, dev(xp, y, z, zc))

        return carry

    for block in range(4):
        project(block, 0)

    @pl.when(owner & (x != y))
    def _():
        wait(res_recv, rsem.at[9])

    @pl.when(owner)
    def _():
        rs1_recv[me] = rs1_send[x * 4 + y]
        wait(rs1_recv.at[pl.ds(0, 31)], rsem.at[5])
        summed = jnp.sum(rs1_recv[...].astype(F32), axis=0)
        xt[zi, y] = (res_recv[...].astype(F32) + summed).astype(BF)

        for _, to in zpeers:
            send(xt.at[zi, y], xt.at[zi, y], 6, to, SX + zi)
        for d in (2, 1, 3):
            send(xt.at[zi, y], xt.at[zi, y], 7, dev(x, ys[d], z, c))
        for cp in range(NC):
            chunk = xt.at[zi, y, pl.ds(cp * 16, 16)]

            @pl.when((x != y) | (c != cp))
            def _():
                send(chunk, str_recv, 12, dev(y, x, z, cp))

            @pl.when((x == y) & (c == cp))
            def _():
                str_recv[...] = chunk[...]

    up = (owner & (zi < 4)) | (jnp.logical_not(owner) & (zi >= 4))
    for j in range(8):
        i = jnp.where(up, j, 7 - j)

        @pl.when(jnp.logical_not(owner) | (i != zi))
        def _():
            wait(xt.at[i, y], rsem.at[SX + i])
            for d in (2, 1, 3):
                send(xt.at[i, y], xt.at[i, y], 7, dev(x, ys[d], z, c))

    own_wg.wait()
    own_gain.wait()
    wait(wg_recv.at[pl.ds(0, 7)], rsem.at[8])

    def scale_gain(i, carry):
        wg_buf[pl.ds(pl.multiple_of(i * 112, 112), 112)] = (wg_recv[i].astype(F32) * gain_buf[...]).astype(BF)
        return carry

    lax.fori_loop(0, NX * NC, scale_gain, 0)

    wait(xt.at[:, pl.ds(0, 3)], rsem.at[7])

    stream = xt[...].reshape(ED, TOK)
    wide = stream.astype(F32)
    squares = jnp.sum(wide * wide, axis=0, keepdims=True)
    high = squares.astype(BF).astype(F32)
    row16 = lax.broadcasted_iota(jnp.int32, (16, TOK), 0)
    both = jnp.where(row16 == 0, high, jnp.where(row16 == 1, squares - high, 0.0)).astype(BF)
    def gate_up_block(i, carry):
        kp = lax.rem(k + 4 + i, NX * NC)
        part = jnp.dot(
            wg_buf[pl.ds(pl.multiple_of(kp * 112, 112), 112)], stream, preferred_element_type=F32
        )
        gsend[kp, pl.ds(0, 112)] = part.astype(BF)
        gsend[kp, pl.ds(112, 16)] = both

        @pl.when(kp != k)
        def _():
            send(gsend.at[kp], grecv.at[k], 13, dev(kp // NC, y, z, kp % NC))

        return carry

    for block in range(8):
        gate_up_block(block, 0)
    grecv[k] = gsend[k]

    own_wd.wait()
    wait(wd_recv.at[pl.ds(0, NY - 1)], rsem.at[11])

    def down_block(i, carry):
        zero = jnp.zeros((HPAD - HID, 128), BF)
        tall = [
            jnp.concatenate([wd_recv[i, pl.ds(n * HID, HID)], zero], axis=0) for n in range(NZ)
        ]
        for n in range(NZ // 2):
            pair = jnp.concatenate([tall[2 * n], tall[2 * n + 1]], axis=0)
            wd_t[pl.ds(pl.multiple_of(i * 128, 128), 128), pl.ds(n * 128, 128)] = pair.T
        return carry

    lax.fori_loop(0, NY, down_block, 0)

    wait(grecv.at[pl.ds(0, 7)], rsem.at[13])
    gu = jnp.sum(grecv[...].astype(F32), axis=0)
    inv_rms = lax.rsqrt((gu[112:113] + gu[113:114]) * (1.0 / (8 * ED)) + norm_eps)
    gate = gu[:HID] * inv_rms
    up = gu[HID : 2 * HID] * inv_rms
    hidden = gate / (1.0 + jnp.exp(-gate)) * up
    ht[z] = jnp.concatenate([hidden, jnp.zeros((HPAD - HID, TOK), F32)], axis=0).astype(BF)

    def zd(d):
        return zs[d % NZ]

    def h_send(block, d, stage):
        send(ht.at[block], ht.at[block], stage, dev(x, y, zd(d), c))

    h_send(z, 5, 16)
    h_send(z, -5, 17)
    h_send(z, 1, 18)
    h_send(z, -1, 19)
    wait(ht.at[0], rsem.at[18])
    h_send(zd(-1), 1, 20)
    wait(ht.at[0], rsem.at[19])
    h_send(zd(1), -1, 21)
    wait(ht.at[0], rsem.at[16])
    h_send(zd(-5), 3, 14)
    h_send(zd(-5), 2, 14)
    h_send(zd(-5), 1, 14)
    h_send(zd(-5), -1, 14)
    wait(ht.at[0], rsem.at[17])
    h_send(zd(5), -2, 14)
    h_send(zd(5), -1, 14)
    h_send(zd(5), 1, 14)
    wait(ht.at[0], rsem.at[20])
    h_send(zd(-2), 1, 14)
    wait(ht.at[0], rsem.at[21])
    h_send(zd(2), -1, 14)
    wait(ht.at[pl.ds(0, 9)], rsem.at[14])

    gathered = ht[...].reshape(NZ * HPAD, TOK)

    def down_project(i, carry):
        yp = ys[(2, 3, 1, 0)[i]]
        down = jnp.dot(
            wd_t[pl.ds(pl.multiple_of(yp * 128, 128), 128)], gathered, preferred_element_type=F32
        )
        rs2_send[pl.ds(yp * 8, 8)] = down.astype(BF).reshape(8, 16, TOK)
        for i in (2, 1, 3):
            for l in range(NC):
                send(rs2_send.at[yp * 8 + xs[i] * 2 + cs[l]], rs2_recv.at[me], 15, dev(xs[i], yp, z, cs[l]))
        send(rs2_send.at[yp * 8 + x * 2 + cs[1]], rs2_recv.at[me], 15, dev(x, yp, z, cs[1]))

        @pl.when(yp != y)
        def _():
            send(rs2_send.at[yp * 8 + k], rs2_recv.at[me], 15, dev(x, yp, z, c))

        return carry

    for block in range(4):
        down_project(block, 0)
    rs2_recv[me] = rs2_send[y * 8 + x * 2 + c]

    @pl.when((x != y) | jnp.logical_not(owner))
    def _():
        wait(str_recv, rsem.at[12])

    wait(ysend.at[pl.ds(0, 3)], ssem.at[0])
    wait(ystat.at[pl.ds(0, 3)], ssem.at[1])
    wait(zsend.at[pl.ds(0, 15)], ssem.at[2])
    wait(zrstat.at[pl.ds(0, 15)], ssem.at[3])
    wait(att.at[pl.ds(0, 15)], ssem.at[4])
    wait(rs1_send.at[pl.ds(0, 15)], ssem.at[5])
    wait(xt.at[:, pl.ds(0, 3)], ssem.at[7])
    wait(wg_recv.at[pl.ds(0, 7)], ssem.at[8])
    wait(wo_recv.at[pl.ds(0, 3)], ssem.at[10])
    wait(wd_recv.at[pl.ds(0, 3)], ssem.at[11])
    wait(gsend.at[pl.ds(0, 7)], ssem.at[13])
    wait(ht.at[pl.ds(0, 9)], ssem.at[14])
    wait(ht.at[0], ssem.at[16])
    wait(ht.at[0], ssem.at[17])
    wait(ht.at[0], ssem.at[18])
    wait(ht.at[0], ssem.at[19])
    wait(ht.at[0], ssem.at[20])
    wait(ht.at[0], ssem.at[21])
    wait(rs2_send.at[pl.ds(0, 31)], ssem.at[15])

    @pl.when(jnp.logical_not(owner))
    def _():
        wait(rs1_send.at[0], ssem.at[5])

    @pl.when(owner)
    def _():
        wait(xt.at[pl.ds(0, 5), pl.ds(0, 3)], ssem.at[6])

    @pl.when(owner & (x != y))
    def _():
        wait(res_recv, ssem.at[9])
        wait(res_recv, ssem.at[12])

    @pl.when(owner & (x == y))
    def _():
        wait(str_recv, ssem.at[12])

    wait(rs2_recv.at[pl.ds(0, 31)], rsem.at[15])
    result = str_recv[...].astype(F32) + jnp.sum(rs2_recv[...].astype(F32), axis=0)
    rounded = result.astype(BF)
    out_ref[0] = rounded[:, :REQ]
    out_ref[1] = rounded[:, REQ:]


def body(
    resid,
    queries,
    new_kv,
    prefix_cache,
    suffix_cache,
    suffix_lengths,
    out_weight,
    norm_gain,
    gate_up,
    down_weight,
):
    hbm = pl.BlockSpec(memory_space=pl.ANY)
    vmem = pltpu.VMEM
    in_vmem = pl.BlockSpec(memory_space=vmem)
    result = pl.pallas_call(
        kernel,
        out_shape=jax.ShapeDtypeStruct((2, 16, REQ), BF),
        in_specs=[hbm] * 10,
        out_specs=in_vmem,
        scratch_shapes=[
            vmem((1, REQ), jnp.int32), vmem((2, 2, DH), BF), vmem((TOK, 128), BF),
            vmem((TOK, HEADS, DH), BF), vmem((TOK * HEADS, DH), F32), vmem((NY, DH, 2 * TOK), BF),
            vmem((KEYS, DH), BF), vmem((KEYS, DH), BF), vmem((DH, KEYS), BF), vmem((2, 8, DH), F32),
            vmem((128, TOK), BF),
            vmem((NY, 256, TOK), BF), vmem((NY, 4, TOK), F32), vmem((NY, 256, TOK), BF), vmem((NY, 4, TOK), F32),
            vmem((NZ, 16, TOK), BF), vmem((2, 1, TOK), F32), vmem((NZ, 16, TOK), BF), vmem((NZ, 1, TOK), F32),
            vmem((NZ, 16, TOK), BF),
            vmem((NY, 256, 128), BF), vmem((512, 256), BF), vmem((16, 32, TOK), BF), vmem((32, 32, TOK), BF),
            vmem((32, TOK), BF),
            vmem((8, NY, 32, TOK), BF), vmem((8, 112, ED), BF), vmem((8 * 112, ED), BF), vmem((1, ED), F32),
            vmem((8, 128, TOK), BF), vmem((8, 128, TOK), BF),
            vmem((NZ, HPAD, TOK), BF), vmem((NY, 896, 128), BF), vmem((512, NZ * HPAD), BF),
            vmem((32, 16, TOK), BF), vmem((32, 16, TOK), BF), vmem((16, TOK), BF),
            pltpu.SemaphoreType.DMA((12,)), pltpu.SemaphoreType.DMA((22,)), pltpu.SemaphoreType.DMA((SX + 8,)),
        ],
        compiler_params=pltpu.CompilerParams(
            collective_id=0, has_side_effects=True, vmem_limit_bytes=63 * 1024 * 1024
        ),
        name="layer",
    )(
        suffix_lengths.reshape(1, REQ), new_kv[:, 0, :, 0, :], resid.reshape(TOK, 128),
        queries.reshape(TOK, HEADS, DH), prefix_cache[:, :, 0, :], suffix_cache[:, 0, :, 0, :],
        out_weight, norm_gain.reshape(8, 1, ED), gate_up[:, :, 0, :].transpose(0, 2, 1).reshape(2 * HID, 8 * ED),
        down_weight,
    )
    return result.transpose(2, 0, 1)


def solution(mesh):
    placed = (
        P(None, None, "seq"),
        P(None, None, "kvh", None),
        P(None, "seq", None, "kvh", None),
        P(None, "seq", "kvh", None),
        P(None, "seq", None, "kvh", None),
        P(),
        P("kvh", "seq"),
        P(),
        P(None, None, "kvh", "seq"),
        P("kvh", "seq"),
    )
    return jax.shard_map(
        body, mesh=mesh, in_specs=placed, out_specs=P(None, None, ("seq", "kvh")), check_vma=False
    )
```

```python
import math

import jax
import jax.numpy as jnp
from jax import lax
from jax.experimental import pallas as pl
from jax.experimental.pallas import tpu as pltpu
from jax.sharding import PartitionSpec as P

theta_base = 500000.0
ntk_factor = 4.0
norm_eps = 1e-05
masked_score = -1e30

MESH = pl.DeviceIdType.MESH
NX, NY, NZ, NC = 4, 4, 16, 2
REQ = 64
TOK = 128
DH = 128
HEADS = 8
PRE, SUF, NEW = 512, 256, 128
KEYS = PRE + SUF + NEW
PREFIX = PRE * NY * NZ
ED = 1024
HID = 56
HPAD = 64
SX = 22
BF, F32 = jnp.bfloat16, jnp.float32
TN = (((0,), (0,)), ((), ()))


def rotary(position, index):
    growth = ntk_factor * (position + 1.0) / float(PREFIX // 4) - (ntk_factor - 1.0)
    log_base = math.log(theta_base) + DH / (DH - 2.0) * jnp.log(growth)
    angles = position * jnp.exp(log_base * (-2.0 * index.astype(F32) / DH))
    return jnp.cos(angles), jnp.sin(angles)


def dev(x, y, z, c):
    return (y * NZ + z, x * NC + c)


def kernel(
    lens_hbm, new_hbm, res_hbm, q_hbm, pre_hbm, suf_hbm, wo_hbm, gain_hbm, wg_hbm, wd_hbm,
    out_ref,
    lens_ref, new_ref, res_ref, q_raw, q_wide, q_buf, k_buf, v_buf, vt_buf, new_buf, res_t,
    ysend, ystat, yrecv, yrstat,
    zsend, zstat, zrecv, zrstat, att,
    wo_recv, wo_t, rs1_send, rs1_recv, res_recv,
    xt, wg_recv, wg_buf, gain_buf, gsend, grecv,
    ht, wd_recv, wd_t, rs2_send, rs2_recv, str_recv,
    loc, ssem, rsem,
):
    s = lax.axis_index("seq")
    k = lax.axis_index("kvh")
    x, c = k // NC, k % NC
    y, z = s // NZ, s % NZ
    zc, zi = z // 8, z % 8
    owner = c == zc

    def send(src, dst, stage, to, at=None):
        at = stage if at is None else at
        copy = pltpu.make_async_remote_copy(
            src_ref=src, dst_ref=dst, send_sem=ssem.at[stage], recv_sem=rsem.at[at],
            device_id=to, device_id_type=MESH,
        )
        copy.start()

    def wait(ref, sem):
        pltpu.make_async_copy(ref, ref, sem).wait()

    xs = [x] + [lax.rem(x + d, NX) for d in range(1, NX)]
    ys = [y] + [lax.rem(y + d, NY) for d in range(1, NY)]
    zs = [z] + [lax.rem(z + d, NZ) for d in range(1, NZ)]
    cs = [c, 1 - c]
    z_order = sorted(range(1, NZ), key=lambda d: -min(d, NZ - d))
    zpeers = [(zs[d], dev(x, y, zs[d], c)) for d in z_order]
    plane = sorted(
        [(i, j, l) for i in range(NX) for j in range(NY) for l in range(NC) if i + j + l],
        key=lambda d: -(min(d[0], NX - d[0]) + min(d[1], NY - d[1])),
    )

    barrier = pltpu.get_barrier_semaphore()

    def greet(to):
        pl.semaphore_signal(barrier, inc=1, device_id=to, device_id_type=MESH)

    for _, to in zpeers:
        greet(to)
    for i, j, l in plane:
        greet(dev(xs[i], ys[j], z, cs[l]))

    load_q = pltpu.make_async_copy(q_hbm, q_raw, loc.at[0])
    load_q.start()
    smalls = [
        pltpu.make_async_copy(lens_hbm, lens_ref, loc.at[9]),
        pltpu.make_async_copy(new_hbm, new_ref, loc.at[10]),
        pltpu.make_async_copy(res_hbm, res_ref, loc.at[11]),
    ]
    for copy in smalls:
        copy.start()
    loads = [
        pltpu.make_async_copy(pre_hbm.at[0], k_buf.at[pl.ds(0, PRE)], loc.at[1]),
        pltpu.make_async_copy(suf_hbm.at[0], k_buf.at[pl.ds(PRE, SUF)], loc.at[2]),
        pltpu.make_async_copy(pre_hbm.at[1], v_buf.at[pl.ds(0, PRE)], loc.at[3]),
        pltpu.make_async_copy(suf_hbm.at[1], v_buf.at[pl.ds(PRE, SUF)], loc.at[4]),
    ]
    for copy in loads:
        copy.start()

    own_wg = pltpu.make_async_copy(wg_hbm.at[:, pl.ds(pl.multiple_of(k * ED, ED), ED)], wg_recv.at[k], loc.at[5])
    own_wo = pltpu.make_async_copy(wo_hbm.at[pl.ds(pl.multiple_of(y * 256, 256), 256)], wo_recv.at[y], loc.at[6])
    own_wd = pltpu.make_async_copy(wd_hbm.at[pl.ds(pl.multiple_of(y * 896, 896), 896)], wd_recv.at[y], loc.at[7])
    own_gain = pltpu.make_async_copy(gain_hbm.at[k], gain_buf, loc.at[8])
    for copy in (own_wg, own_wo, own_wd, own_gain):
        copy.start()

    for copy in smalls:
        copy.wait()
    lens = lens_ref[...]
    position = (PREFIX + jnp.concatenate([lens, lens + 1], axis=1)).astype(F32)
    cos, sin = rotary(position, lax.broadcasted_iota(jnp.int32, (DH // 2, TOK), 0))
    token = lax.broadcasted_iota(jnp.int32, (TOK, TOK), 0)
    place = lax.broadcasted_iota(jnp.int32, (TOK, TOK), 1)
    perm = (token == 2 * (place % REQ) + place // REQ).astype(F32).astype(BF)
    load_q.wait()
    q_wide[...] = q_raw[...].astype(F32).reshape(TOK * HEADS, DH)
    for h in range(HEADS):
        rows = q_wide[pl.ds(h, TOK, stride=HEADS)].astype(BF)
        turned = lax.dot_general(rows, perm, TN, preferred_element_type=F32)
        a, b = turned[: DH // 2], turned[DH // 2 :]
        q_buf[h // 2, :, pl.ds((h % 2) * TOK, TOK)] = jnp.concatenate(
            [a * cos - b * sin, b * cos + a * sin], axis=0
        ).astype(BF)

    own = lax.broadcasted_iota(jnp.int32, (1, REQ), 1) == s
    length = jnp.sum(jnp.where(own, lens.astype(F32), 0.0), axis=1, keepdims=True)
    lane8 = lax.broadcasted_iota(jnp.int32, (8, DH), 1)
    row8 = lax.broadcasted_iota(jnp.int32, (8, DH), 0)
    cos8, sin8 = rotary(PREFIX + length + row8.astype(F32), lane8 % (DH // 2))
    new_buf[...] = jnp.zeros_like(new_buf)
    new_buf[0, pl.ds(0, 2)] = new_ref[0].astype(F32)
    new_buf[1, pl.ds(0, 2)] = new_ref[1].astype(F32)
    fresh = new_buf[0]
    other = pltpu.roll(fresh, DH // 2, 1)
    fresh = fresh * cos8 + jnp.where(lane8 < DH // 2, -other, other) * sin8
    none = jnp.zeros((NEW - 8, DH), F32)
    k_buf[pl.ds(PRE + SUF, NEW)] = jnp.concatenate([fresh, none], axis=0).astype(BF)
    v_buf[pl.ds(PRE + SUF, NEW)] = jnp.concatenate([new_buf[1], none], axis=0).astype(BF)
    for copy in loads:
        copy.wait()
    vt_buf[...] = v_buf[...].T
    row = lax.broadcasted_iota(jnp.int32, (SUF + NEW, 2 * TOK), 0)
    lane = lax.broadcasted_iota(jnp.int32, (SUF + NEW, 2 * TOK), 1)
    live = (lane % REQ == s) & ((row.astype(F32) < length) | ((row >= SUF) & (row - SUF <= (lane // REQ) % 2)))
    scale = 1.0 / math.sqrt(DH)

    def attend(dst, stat, yq):
        raw = jnp.dot(k_buf[...], q_buf[yq], preferred_element_type=F32) * scale
        first = raw[:PRE]
        second = jnp.where(live, raw[PRE:], masked_score)
        peak = jnp.maximum(
            jnp.max(first, axis=0, keepdims=True), jnp.max(second, axis=0, keepdims=True)
        )
        e1 = jnp.exp(first - peak)
        e2 = jnp.exp(second - peak)
        total = jnp.sum(e1, axis=0, keepdims=True) + jnp.sum(e2, axis=0, keepdims=True)
        acc = jnp.dot(vt_buf[:, :PRE], e1.astype(BF), preferred_element_type=F32)
        acc = acc + jnp.dot(vt_buf[:, PRE:], e2.astype(BF), preferred_element_type=F32)
        for h in range(2):
            dst[pl.ds(h * DH, DH)] = acc[:, h * TOK : (h + 1) * TOK].astype(BF)
            stat[pl.ds(2 * h, 1)] = peak[:, h * TOK : (h + 1) * TOK]
            stat[pl.ds(2 * h + 1, 1)] = total[:, h * TOK : (h + 1) * TOK]

    def y_send(yp):
        send(ysend.at[yp], yrecv.at[y], 0, dev(x, yp, z, c))
        send(ystat.at[yp], yrstat.at[y], 1, dev(x, yp, z, c))

    def attend_block(i, carry):
        yq = lax.rem(y + 1 + i, NY)
        attend(ysend.at[yq], ystat.at[yq], yq)
        return carry

    lax.fori_loop(0, NY - 1, attend_block, 0)
    pl.semaphore_wait(barrier, 46)
    for d in (2, 1, 3):
        y_send(ys[d])

    def wg_rows(n, carry):
        rows = pl.ds(pl.multiple_of(n * 16, 16), 16)
        for i in (2, 1, 3, 0):
            for l in range(NC):
                if i + l:
                    lanes = pl.ds(pl.multiple_of((xs[i] * NC + cs[l]) * ED, ED), ED)
                    send(wg_hbm.at[rows, lanes], wg_recv.at[k, rows], 8, dev(xs[i], y, z, cs[l]))
        return carry

    lax.fori_loop(0, 7, wg_rows, 0)
    res_t[...] = lax.dot_general(res_ref[...], perm, TN, preferred_element_type=F32).astype(BF)

    @pl.when(owner & (x != y))
    def _():
        send(res_t.at[pl.ds(pl.multiple_of(x * 32, 32), 32)], res_recv, 9, dev(y, x, z, c))

    @pl.when(owner & (x == y))
    def _():
        res_recv[...] = res_t[pl.ds(pl.multiple_of(x * 32, 32), 32)]

    attend(yrecv.at[y], yrstat.at[y], y)
    wait(yrecv.at[pl.ds(0, NY - 1)], rsem.at[0])
    wait(yrstat.at[pl.ds(0, NY - 1)], rsem.at[1])

    for h in range(2):
        peaks = [yrstat[i, pl.ds(2 * h, 1)] for i in range(NY)]
        joint = jnp.maximum(jnp.maximum(peaks[0], peaks[1]), jnp.maximum(peaks[2], peaks[3]))
        facs = [jnp.exp(p - joint) for p in peaks]
        total = sum(yrstat[i, pl.ds(2 * h + 1, 1)] * facs[i] for i in range(NY))
        acc = sum(yrecv[i, pl.ds(h * DH, DH)].astype(F32) * facs[i] for i in range(NY))
        zsend[pl.ds(h * 8, 8)] = (acc / total).astype(BF).reshape(8, 16, TOK)
        zstat[h] = joint + jnp.log(total)

    for zp, to in zpeers:
        send(zstat.at[zp // 8], zrstat.at[z], 3, to)
        send(zsend.at[zp], zrecv.at[z], 2, to)

    for d in (2, 1, 3):
        send(
            wo_hbm.at[pl.ds(pl.multiple_of(ys[d] * 256, 256), 256)], wo_recv.at[y], 10, dev(x, ys[d], z, c)
        )
    for d in (2, 1, 3):
        send(
            wd_hbm.at[pl.ds(pl.multiple_of(ys[d] * 896, 896), 896)], wd_recv.at[y], 11, dev(x, ys[d], z, c)
        )
    zrecv[z] = zsend[z]
    zrstat[z] = zstat[z // 8]
    wait(zrstat.at[pl.ds(0, NZ - 1)], rsem.at[3])
    wait(zrecv.at[pl.ds(0, NZ - 1)], rsem.at[2])

    logs = zrstat[...].reshape(NZ, TOK)
    facs = jnp.exp(logs - jnp.max(logs, axis=0, keepdims=True))
    acc = jnp.sum(zrecv[...].astype(F32) * facs[:, None, :], axis=0)
    att[z] = (acc / jnp.sum(facs, axis=0, keepdims=True)).astype(BF)

    for _, to in zpeers:
        send(att.at[z], att.at[z], 4, to)

    own_wo.wait()
    wait(wo_recv.at[pl.ds(0, NY - 1)], rsem.at[10])
    for i in range(NY):
        wo_t[pl.ds(i * 128, 128)] = wo_recv[i].T
    wait(att.at[pl.ds(0, NZ - 1)], rsem.at[4])

    me = x * 8 + y * 2 + c
    spread = att[...].reshape(256, TOK)

    def project(i, carry):
        xp = xs[(2, 3, 1, 0)[i]]
        rows = pl.ds(pl.multiple_of(xp * 128, 128), 128)
        proj = jnp.dot(wo_t[rows], spread, preferred_element_type=F32)
        rs1_send[pl.ds(xp * 4, 4)] = proj.astype(BF).reshape(4, 32, TOK)
        for j in (2, 1, 3):
            send(rs1_send.at[xp * 4 + ys[j]], rs1_recv.at[me], 5, dev(xp, ys[j], z, zc))

        @pl.when((xp != x) | jnp.logical_not(owner))
        def _():
            send(rs1_send.at[xp * 4 + y], rs1_recv.at[me], 5, dev(xp, y, z, zc))

        return carry

    for block in range(4):
        project(block, 0)

    @pl.when(owner & (x != y))
    def _():
        wait(res_recv, rsem.at[9])

    @pl.when(owner)
    def _():
        rs1_recv[me] = rs1_send[x * 4 + y]
        wait(rs1_recv.at[pl.ds(0, 31)], rsem.at[5])
        summed = jnp.sum(rs1_recv[...].astype(F32), axis=0)
        xt[zi, y] = (res_recv[...].astype(F32) + summed).astype(BF)

        for _, to in zpeers:
            send(xt.at[zi, y], xt.at[zi, y], 6, to, SX + zi)
        for d in (2, 1, 3):
            send(xt.at[zi, y], xt.at[zi, y], 7, dev(x, ys[d], z, c))
        for cp in range(NC):
            chunk = xt.at[zi, y, pl.ds(cp * 16, 16)]

            @pl.when((x != y) | (c != cp))
            def _():
                send(chunk, str_recv, 12, dev(y, x, z, cp))

            @pl.when((x == y) & (c == cp))
            def _():
                str_recv[...] = chunk[...]

    up = (owner & (zi < 4)) | (jnp.logical_not(owner) & (zi >= 4))
    for j in range(8):
        i = jnp.where(up, j, 7 - j)

        @pl.when(jnp.logical_not(owner) | (i != zi))
        def _():
            wait(xt.at[i, y], rsem.at[SX + i])
            for d in (2, 1, 3):
                send(xt.at[i, y], xt.at[i, y], 7, dev(x, ys[d], z, c))

    own_wg.wait()
    own_gain.wait()
    wait(wg_recv.at[pl.ds(0, 7)], rsem.at[8])

    def scale_gain(i, carry):
        wg_buf[pl.ds(pl.multiple_of(i * 112, 112), 112)] = (wg_recv[i].astype(F32) * gain_buf[...]).astype(BF)
        return carry

    lax.fori_loop(0, NX * NC, scale_gain, 0)

    wait(xt.at[:, pl.ds(0, 3)], rsem.at[7])

    stream = xt[...].reshape(ED, TOK)
    wide = stream.astype(F32)
    squares = jnp.sum(wide * wide, axis=0, keepdims=True)
    high = squares.astype(BF).astype(F32)
    row16 = lax.broadcasted_iota(jnp.int32, (16, TOK), 0)
    both = jnp.where(row16 == 0, high, jnp.where(row16 == 1, squares - high, 0.0)).astype(BF)
    def gate_up_block(i, carry):
        kp = xs[(2, 2, 1, 1, 3, 3, 0, 0)[i]] * NC + cs[(0, 1, 0, 1, 0, 1, 1, 0)[i]]
        part = jnp.dot(
            wg_buf[pl.ds(pl.multiple_of(kp * 112, 112), 112)], stream, preferred_element_type=F32
        )
        gsend[kp, pl.ds(0, 112)] = part.astype(BF)
        gsend[kp, pl.ds(112, 16)] = both

        if i < 7:
            to = dev(xs[(2, 2, 1, 1, 3, 3, 0)[i]], y, z, cs[(0, 1, 0, 1, 0, 1, 1)[i]])
            send(gsend.at[kp], grecv.at[k], 13, to)

        return carry

    for block in range(8):
        gate_up_block(block, 0)
    grecv[k] = gsend[k]

    own_wd.wait()
    wait(wd_recv.at[pl.ds(0, NY - 1)], rsem.at[11])

    def down_block(i, carry):
        zero = jnp.zeros((HPAD - HID, 128), BF)
        tall = [
            jnp.concatenate([wd_recv[i, pl.ds(n * HID, HID)], zero], axis=0) for n in range(NZ)
        ]
        for n in range(NZ // 2):
            pair = jnp.concatenate([tall[2 * n], tall[2 * n + 1]], axis=0)
            wd_t[pl.ds(pl.multiple_of(i * 128, 128), 128), pl.ds(n * 128, 128)] = pair.T
        return carry

    lax.fori_loop(0, NY, down_block, 0)

    wait(grecv.at[pl.ds(0, 7)], rsem.at[13])
    gu = jnp.sum(grecv[...].astype(F32), axis=0)
    inv_rms = lax.rsqrt((gu[112:113] + gu[113:114]) * (1.0 / (8 * ED)) + norm_eps)
    gate = gu[:HID] * inv_rms
    up = gu[HID : 2 * HID] * inv_rms
    hidden = gate / (1.0 + jnp.exp(-gate)) * up
    ht[z] = jnp.concatenate([hidden, jnp.zeros((HPAD - HID, TOK), F32)], axis=0).astype(BF)

    def zd(d):
        return zs[d % NZ]

    def h_send(block, d, stage):
        send(ht.at[block], ht.at[block], stage, dev(x, y, zd(d), c))

    h_send(z, 5, 16)
    h_send(z, -5, 17)
    h_send(z, 1, 18)
    h_send(z, -1, 19)
    wait(ht.at[0], rsem.at[18])
    h_send(zd(-1), 1, 20)
    wait(ht.at[0], rsem.at[19])
    h_send(zd(1), -1, 21)
    wait(ht.at[0], rsem.at[16])
    h_send(zd(-5), 3, 14)
    h_send(zd(-5), 2, 14)
    h_send(zd(-5), 1, 14)
    h_send(zd(-5), -1, 14)
    wait(ht.at[0], rsem.at[17])
    h_send(zd(5), -2, 14)
    h_send(zd(5), -1, 14)
    h_send(zd(5), 1, 14)
    wait(ht.at[0], rsem.at[20])
    h_send(zd(-2), 1, 14)
    wait(ht.at[0], rsem.at[21])
    h_send(zd(2), -1, 14)
    wait(ht.at[pl.ds(0, 9)], rsem.at[14])

    gathered = ht[...].reshape(NZ * HPAD, TOK)

    def down_project(i, carry):
        yp = ys[(2, 3, 1, 0)[i]]
        down = jnp.dot(
            wd_t[pl.ds(pl.multiple_of(yp * 128, 128), 128)], gathered, preferred_element_type=F32
        )
        rs2_send[pl.ds(yp * 8, 8)] = down.astype(BF).reshape(8, 16, TOK)
        for i in (2, 1, 3):
            for l in range(NC):
                send(rs2_send.at[yp * 8 + xs[i] * 2 + cs[l]], rs2_recv.at[me], 15, dev(xs[i], yp, z, cs[l]))
        send(rs2_send.at[yp * 8 + x * 2 + cs[1]], rs2_recv.at[me], 15, dev(x, yp, z, cs[1]))

        @pl.when(yp != y)
        def _():
            send(rs2_send.at[yp * 8 + k], rs2_recv.at[me], 15, dev(x, yp, z, c))

        return carry

    for block in range(4):
        down_project(block, 0)
    rs2_recv[me] = rs2_send[y * 8 + x * 2 + c]

    @pl.when((x != y) | jnp.logical_not(owner))
    def _():
        wait(str_recv, rsem.at[12])

    wait(ysend.at[pl.ds(0, 3)], ssem.at[0])
    wait(ystat.at[pl.ds(0, 3)], ssem.at[1])
    wait(zsend.at[pl.ds(0, 15)], ssem.at[2])
    wait(zrstat.at[pl.ds(0, 15)], ssem.at[3])
    wait(att.at[pl.ds(0, 15)], ssem.at[4])
    wait(rs1_send.at[pl.ds(0, 15)], ssem.at[5])
    wait(xt.at[:, pl.ds(0, 3)], ssem.at[7])
    wait(wg_recv.at[pl.ds(0, 7)], ssem.at[8])
    wait(wo_recv.at[pl.ds(0, 3)], ssem.at[10])
    wait(wd_recv.at[pl.ds(0, 3)], ssem.at[11])
    wait(gsend.at[pl.ds(0, 7)], ssem.at[13])
    wait(ht.at[pl.ds(0, 9)], ssem.at[14])
    wait(ht.at[0], ssem.at[16])
    wait(ht.at[0], ssem.at[17])
    wait(ht.at[0], ssem.at[18])
    wait(ht.at[0], ssem.at[19])
    wait(ht.at[0], ssem.at[20])
    wait(ht.at[0], ssem.at[21])
    wait(rs2_send.at[pl.ds(0, 31)], ssem.at[15])

    @pl.when(jnp.logical_not(owner))
    def _():
        wait(rs1_send.at[0], ssem.at[5])

    @pl.when(owner)
    def _():
        wait(xt.at[pl.ds(0, 5), pl.ds(0, 3)], ssem.at[6])

    @pl.when(owner & (x != y))
    def _():
        wait(res_recv, ssem.at[9])
        wait(res_recv, ssem.at[12])

    @pl.when(owner & (x == y))
    def _():
        wait(str_recv, ssem.at[12])

    wait(rs2_recv.at[pl.ds(0, 31)], rsem.at[15])
    result = str_recv[...].astype(F32) + jnp.sum(rs2_recv[...].astype(F32), axis=0)
    rounded = result.astype(BF)
    out_ref[0] = rounded[:, :REQ]
    out_ref[1] = rounded[:, REQ:]


def body(
    resid,
    queries,
    new_kv,
    prefix_cache,
    suffix_cache,
    suffix_lengths,
    out_weight,
    norm_gain,
    gate_up,
    down_weight,
):
    hbm = pl.BlockSpec(memory_space=pl.ANY)
    vmem = pltpu.VMEM
    in_vmem = pl.BlockSpec(memory_space=vmem)
    result = pl.pallas_call(
        kernel,
        out_shape=jax.ShapeDtypeStruct((2, 16, REQ), BF),
        in_specs=[hbm] * 10,
        out_specs=in_vmem,
        scratch_shapes=[
            vmem((1, REQ), jnp.int32), vmem((2, 2, DH), BF), vmem((TOK, 128), BF),
            vmem((TOK, HEADS, DH), BF), vmem((TOK * HEADS, DH), F32), vmem((NY, DH, 2 * TOK), BF),
            vmem((KEYS, DH), BF), vmem((KEYS, DH), BF), vmem((DH, KEYS), BF), vmem((2, 8, DH), F32),
            vmem((128, TOK), BF),
            vmem((NY, 256, TOK), BF), vmem((NY, 4, TOK), F32), vmem((NY, 256, TOK), BF), vmem((NY, 4, TOK), F32),
            vmem((NZ, 16, TOK), BF), vmem((2, 1, TOK), F32), vmem((NZ, 16, TOK), BF), vmem((NZ, 1, TOK), F32),
            vmem((NZ, 16, TOK), BF),
            vmem((NY, 256, 128), BF), vmem((512, 256), BF), vmem((16, 32, TOK), BF), vmem((32, 32, TOK), BF),
            vmem((32, TOK), BF),
            vmem((8, NY, 32, TOK), BF), vmem((8, 112, ED), BF), vmem((8 * 112, ED), BF), vmem((1, ED), F32),
            vmem((8, 128, TOK), BF), vmem((8, 128, TOK), BF),
            vmem((NZ, HPAD, TOK), BF), vmem((NY, 896, 128), BF), vmem((512, NZ * HPAD), BF),
            vmem((32, 16, TOK), BF), vmem((32, 16, TOK), BF), vmem((16, TOK), BF),
            pltpu.SemaphoreType.DMA((12,)), pltpu.SemaphoreType.DMA((22,)), pltpu.SemaphoreType.DMA((SX + 8,)),
        ],
        compiler_params=pltpu.CompilerParams(
            collective_id=0, has_side_effects=True, vmem_limit_bytes=63 * 1024 * 1024
        ),
        name="layer",
    )(
        suffix_lengths.reshape(1, REQ), new_kv[:, 0, :, 0, :], resid.reshape(TOK, 128),
        queries.reshape(TOK, HEADS, DH), prefix_cache[:, :, 0, :], suffix_cache[:, 0, :, 0, :],
        out_weight, norm_gain.reshape(8, 1, ED), gate_up[:, :, 0, :].transpose(0, 2, 1).reshape(2 * HID, 8 * ED),
        down_weight,
    )
    return result.transpose(2, 0, 1)


def solution(mesh):
    placed = (
        P(None, None, "seq"),
        P(None, None, "kvh", None),
        P(None, "seq", None, "kvh", None),
        P(None, "seq", "kvh", None),
        P(None, "seq", None, "kvh", None),
        P(),
        P("kvh", "seq"),
        P(),
        P(None, None, "kvh", "seq"),
        P("kvh", "seq"),
    )
    return jax.shard_map(
        body, mesh=mesh, in_specs=placed, out_specs=P(None, None, ("seq", "kvh")), check_vma=False
    )
```

```python
import math

import jax
import jax.numpy as jnp
from jax import lax
from jax.experimental import pallas as pl
from jax.experimental.pallas import tpu as pltpu
from jax.sharding import PartitionSpec as P

theta_base = 500000.0
ntk_factor = 4.0
norm_eps = 1e-05
masked_score = -1e30

MESH = pl.DeviceIdType.MESH
NX, NY, NZ, NC = 4, 4, 16, 2
REQ = 64
TOK = 128
DH = 128
HEADS = 8
PRE, SUF, NEW = 512, 256, 128
KEYS = PRE + SUF + NEW
PREFIX = PRE * NY * NZ
ED = 1024
HID = 56
HPAD = 64
SX = 22
BF, F32 = jnp.bfloat16, jnp.float32
TN = (((0,), (0,)), ((), ()))


def rotary(position, index):
    growth = ntk_factor * (position + 1.0) / float(PREFIX // 4) - (ntk_factor - 1.0)
    log_base = math.log(theta_base) + DH / (DH - 2.0) * jnp.log(growth)
    angles = position * jnp.exp(log_base * (-2.0 * index.astype(F32) / DH))
    return jnp.cos(angles), jnp.sin(angles)


def dev(x, y, z, c):
    return (y * NZ + z, x * NC + c)


def kernel(
    lens_hbm, new_hbm, res_hbm, q_hbm, pre_hbm, suf_hbm, wo_hbm, gain_hbm, wg_hbm, wd_hbm,
    out_ref,
    lens_ref, new_ref, res_ref, q_raw, q_wide, q_buf, k_buf, v_buf, vt_buf, new_buf, res_t,
    ysend, ystat, yrecv, yrstat,
    zsend, zstat, zrecv, zrstat, att,
    wo_recv, wo_t, rs1_send, rs1_recv, res_recv,
    xt, wg_recv, wg_buf, gain_buf, gsend, grecv,
    ht, wd_recv, wd_t, rs2_send, rs2_recv, str_recv,
    loc, ssem, rsem,
):
    s = lax.axis_index("seq")
    k = lax.axis_index("kvh")
    x, c = k // NC, k % NC
    y, z = s // NZ, s % NZ
    zc, zi = z // 8, z % 8
    owner = c == zc

    def send(src, dst, stage, to, at=None):
        at = stage if at is None else at
        copy = pltpu.make_async_remote_copy(
            src_ref=src, dst_ref=dst, send_sem=ssem.at[stage], recv_sem=rsem.at[at],
            device_id=to, device_id_type=MESH,
        )
        copy.start()

    def wait(ref, sem):
        pltpu.make_async_copy(ref, ref, sem).wait()

    xs = [x] + [lax.rem(x + d, NX) for d in range(1, NX)]
    ys = [y] + [lax.rem(y + d, NY) for d in range(1, NY)]
    zs = [z] + [lax.rem(z + d, NZ) for d in range(1, NZ)]
    cs = [c, 1 - c]
    z_order = sorted(range(1, NZ), key=lambda d: -min(d, NZ - d))
    zpeers = [(zs[d], dev(x, y, zs[d], c)) for d in z_order]
    plane = sorted(
        [(i, j, l) for i in range(NX) for j in range(NY) for l in range(NC) if i + j + l],
        key=lambda d: -(min(d[0], NX - d[0]) + min(d[1], NY - d[1])),
    )

    barrier = pltpu.get_barrier_semaphore()

    def greet(to):
        pl.semaphore_signal(barrier, inc=1, device_id=to, device_id_type=MESH)

    for _, to in zpeers:
        greet(to)
    for i, j, l in plane:
        greet(dev(xs[i], ys[j], z, cs[l]))

    load_q = pltpu.make_async_copy(q_hbm, q_raw, loc.at[0])
    load_q.start()
    smalls = [
        pltpu.make_async_copy(lens_hbm, lens_ref, loc.at[9]),
        pltpu.make_async_copy(new_hbm, new_ref, loc.at[10]),
        pltpu.make_async_copy(res_hbm, res_ref, loc.at[11]),
    ]
    for copy in smalls:
        copy.start()
    loads = [
        pltpu.make_async_copy(pre_hbm.at[0], k_buf.at[pl.ds(0, PRE)], loc.at[1]),
        pltpu.make_async_copy(suf_hbm.at[0], k_buf.at[pl.ds(PRE, SUF)], loc.at[2]),
        pltpu.make_async_copy(pre_hbm.at[1], v_buf.at[pl.ds(0, PRE)], loc.at[3]),
        pltpu.make_async_copy(suf_hbm.at[1], v_buf.at[pl.ds(PRE, SUF)], loc.at[4]),
    ]
    for copy in loads:
        copy.start()

    own_wg = pltpu.make_async_copy(wg_hbm.at[:, pl.ds(pl.multiple_of(k * ED, ED), ED)], wg_recv.at[k], loc.at[5])
    own_wo = pltpu.make_async_copy(wo_hbm.at[pl.ds(pl.multiple_of(y * 256, 256), 256)], wo_recv.at[y], loc.at[6])
    own_wd = pltpu.make_async_copy(wd_hbm.at[pl.ds(pl.multiple_of(y * 896, 896), 896)], wd_recv.at[y], loc.at[7])
    own_gain = pltpu.make_async_copy(gain_hbm.at[k], gain_buf, loc.at[8])
    for copy in (own_wg, own_wo, own_wd, own_gain):
        copy.start()

    for copy in smalls:
        copy.wait()
    lens = lens_ref[...]
    position = (PREFIX + jnp.concatenate([lens, lens + 1], axis=1)).astype(F32)
    cos, sin = rotary(position, lax.broadcasted_iota(jnp.int32, (DH // 2, TOK), 0))
    token = lax.broadcasted_iota(jnp.int32, (TOK, TOK), 0)
    place = lax.broadcasted_iota(jnp.int32, (TOK, TOK), 1)
    perm = (token == 2 * (place % REQ) + place // REQ).astype(F32).astype(BF)
    load_q.wait()
    q_wide[...] = q_raw[...].astype(F32).reshape(TOK * HEADS, DH)
    for h in range(HEADS):
        rows = q_wide[pl.ds(h, TOK, stride=HEADS)].astype(BF)
        turned = lax.dot_general(rows, perm, TN, preferred_element_type=F32)
        a, b = turned[: DH // 2], turned[DH // 2 :]
        q_buf[h // 2, :, pl.ds((h % 2) * TOK, TOK)] = jnp.concatenate(
            [a * cos - b * sin, b * cos + a * sin], axis=0
        ).astype(BF)

    own = lax.broadcasted_iota(jnp.int32, (1, REQ), 1) == s
    length = jnp.sum(jnp.where(own, lens.astype(F32), 0.0), axis=1, keepdims=True)
    lane8 = lax.broadcasted_iota(jnp.int32, (8, DH), 1)
    row8 = lax.broadcasted_iota(jnp.int32, (8, DH), 0)
    cos8, sin8 = rotary(PREFIX + length + row8.astype(F32), lane8 % (DH // 2))
    new_buf[...] = jnp.zeros_like(new_buf)
    new_buf[0, pl.ds(0, 2)] = new_ref[0].astype(F32)
    new_buf[1, pl.ds(0, 2)] = new_ref[1].astype(F32)
    fresh = new_buf[0]
    other = pltpu.roll(fresh, DH // 2, 1)
    fresh = fresh * cos8 + jnp.where(lane8 < DH // 2, -other, other) * sin8
    none = jnp.zeros((NEW - 8, DH), F32)
    k_buf[pl.ds(PRE + SUF, NEW)] = jnp.concatenate([fresh, none], axis=0).astype(BF)
    v_buf[pl.ds(PRE + SUF, NEW)] = jnp.concatenate([new_buf[1], none], axis=0).astype(BF)
    for copy in loads:
        copy.wait()
    vt_buf[...] = v_buf[...].T
    row = lax.broadcasted_iota(jnp.int32, (SUF + NEW, 2 * TOK), 0)
    lane = lax.broadcasted_iota(jnp.int32, (SUF + NEW, 2 * TOK), 1)
    live = (lane % REQ == s) & ((row.astype(F32) < length) | ((row >= SUF) & (row - SUF <= (lane // REQ) % 2)))
    scale = 1.0 / math.sqrt(DH)

    def attend(dst, stat, yq):
        raw = jnp.dot(k_buf[...], q_buf[yq], preferred_element_type=F32) * scale
        first = raw[:PRE]
        second = jnp.where(live, raw[PRE:], masked_score)
        peak = jnp.maximum(
            jnp.max(first, axis=0, keepdims=True), jnp.max(second, axis=0, keepdims=True)
        )
        e1 = jnp.exp(first - peak)
        e2 = jnp.exp(second - peak)
        total = jnp.sum(e1, axis=0, keepdims=True) + jnp.sum(e2, axis=0, keepdims=True)
        acc = jnp.dot(vt_buf[:, :PRE], e1.astype(BF), preferred_element_type=F32)
        acc = acc + jnp.dot(vt_buf[:, PRE:], e2.astype(BF), preferred_element_type=F32)
        for h in range(2):
            dst[pl.ds(h * DH, DH)] = acc[:, h * TOK : (h + 1) * TOK].astype(BF)
            stat[pl.ds(2 * h, 1)] = peak[:, h * TOK : (h + 1) * TOK]
            stat[pl.ds(2 * h + 1, 1)] = total[:, h * TOK : (h + 1) * TOK]


    def attend_block(i, carry):
        yq = lax.rem(y + 1 + i, NY)
        attend(ysend.at[yq], ystat.at[yq], yq)
        return carry

    lax.fori_loop(0, NY - 1, attend_block, 0)
    pl.semaphore_wait(barrier, 46)
    for d in (2, 1, 3):
        send(ysend.at[ys[d]], yrecv.at[y], 0, dev(x, ys[d], z, c))
    for d in (2, 1, 3):
        send(ystat.at[ys[d]], yrstat.at[y], 1, dev(x, ys[d], z, c))

    def wg_rows(n, carry):
        rows = pl.ds(pl.multiple_of(n * 16, 16), 16)
        for i in (2, 1, 3, 0):
            for l in range(NC):
                if i + l:
                    lanes = pl.ds(pl.multiple_of((xs[i] * NC + cs[l]) * ED, ED), ED)
                    send(wg_hbm.at[rows, lanes], wg_recv.at[k, rows], 8, dev(xs[i], y, z, cs[l]))
        return carry

    lax.fori_loop(0, 7, wg_rows, 0)
    res_t[...] = lax.dot_general(res_ref[...], perm, TN, preferred_element_type=F32).astype(BF)

    @pl.when(owner & (x != y))
    def _():
        send(res_t.at[pl.ds(pl.multiple_of(x * 32, 32), 32)], res_recv, 9, dev(y, x, z, c))

    @pl.when(owner & (x == y))
    def _():
        res_recv[...] = res_t[pl.ds(pl.multiple_of(x * 32, 32), 32)]

    attend(yrecv.at[y], yrstat.at[y], y)
    wait(yrecv.at[pl.ds(0, NY - 1)], rsem.at[0])
    wait(yrstat.at[pl.ds(0, NY - 1)], rsem.at[1])

    for h in range(2):
        peaks = [yrstat[i, pl.ds(2 * h, 1)] for i in range(NY)]
        joint = jnp.maximum(jnp.maximum(peaks[0], peaks[1]), jnp.maximum(peaks[2], peaks[3]))
        facs = [jnp.exp(p - joint) for p in peaks]
        total = sum(yrstat[i, pl.ds(2 * h + 1, 1)] * facs[i] for i in range(NY))
        acc = sum(yrecv[i, pl.ds(h * DH, DH)].astype(F32) * facs[i] for i in range(NY))
        zsend[pl.ds(h * 8, 8)] = (acc / total).astype(BF).reshape(8, 16, TOK)
        zstat[h] = joint + jnp.log(total)

    for zp, to in zpeers:
        send(zsend.at[zp], zrecv.at[z], 2, to)
        send(zstat.at[zp // 8], zrstat.at[z], 3, to)

    for d in (2, 1, 3):
        send(
            wo_hbm.at[pl.ds(pl.multiple_of(ys[d] * 256, 256), 256)], wo_recv.at[y], 10, dev(x, ys[d], z, c)
        )
    for d in (2, 1, 3):
        send(
            wd_hbm.at[pl.ds(pl.multiple_of(ys[d] * 896, 896), 896)], wd_recv.at[y], 11, dev(x, ys[d], z, c)
        )
    zrecv[z] = zsend[z]
    zrstat[z] = zstat[z // 8]
    wait(zrstat.at[pl.ds(0, NZ - 1)], rsem.at[3])
    wait(zrecv.at[pl.ds(0, NZ - 1)], rsem.at[2])

    logs = zrstat[...].reshape(NZ, TOK)
    facs = jnp.exp(logs - jnp.max(logs, axis=0, keepdims=True))
    acc = jnp.sum(zrecv[...].astype(F32) * facs[:, None, :], axis=0)
    att[z] = (acc / jnp.sum(facs, axis=0, keepdims=True)).astype(BF)

    for _, to in zpeers:
        send(att.at[z], att.at[z], 4, to)

    own_wo.wait()
    wait(wo_recv.at[pl.ds(0, NY - 1)], rsem.at[10])
    for i in range(NY):
        wo_t[pl.ds(i * 128, 128)] = wo_recv[i].T
    wait(att.at[pl.ds(0, NZ - 1)], rsem.at[4])

    me = x * 8 + y * 2 + c
    spread = att[...].reshape(256, TOK)

    def project(i, carry):
        xp = xs[(2, 3, 1, 0)[i]]
        rows = pl.ds(pl.multiple_of(xp * 128, 128), 128)
        proj = jnp.dot(wo_t[rows], spread, preferred_element_type=F32)
        rs1_send[pl.ds(xp * 4, 4)] = proj.astype(BF).reshape(4, 32, TOK)
        for j in (2, 1, 3):
            send(rs1_send.at[xp * 4 + ys[j]], rs1_recv.at[me], 5, dev(xp, ys[j], z, zc))

        @pl.when((xp != x) | jnp.logical_not(owner))
        def _():
            send(rs1_send.at[xp * 4 + y], rs1_recv.at[me], 5, dev(xp, y, z, zc))

        return carry

    for block in range(4):
        project(block, 0)

    @pl.when(owner & (x != y))
    def _():
        wait(res_recv, rsem.at[9])

    @pl.when(owner)
    def _():
        rs1_recv[me] = rs1_send[x * 4 + y]
        wait(rs1_recv.at[pl.ds(0, 31)], rsem.at[5])
        summed = jnp.sum(rs1_recv[...].astype(F32), axis=0)
        xt[zi, y] = (res_recv[...].astype(F32) + summed).astype(BF)

        for _, to in zpeers:
            send(xt.at[zi, y], xt.at[zi, y], 6, to, SX + zi)
        for d in (2, 1, 3):
            send(xt.at[zi, y], xt.at[zi, y], 7, dev(x, ys[d], z, c))
        for cp in range(NC):
            chunk = xt.at[zi, y, pl.ds(cp * 16, 16)]

            @pl.when((x != y) | (c != cp))
            def _():
                send(chunk, str_recv, 12, dev(y, x, z, cp))

            @pl.when((x == y) & (c == cp))
            def _():
                str_recv[...] = chunk[...]

    up = (owner & (zi < 4)) | (jnp.logical_not(owner) & (zi >= 4))
    for j in range(8):
        i = jnp.where(up, j, 7 - j)

        @pl.when(jnp.logical_not(owner) | (i != zi))
        def _():
            wait(xt.at[i, y], rsem.at[SX + i])
            for d in (2, 1, 3):
                send(xt.at[i, y], xt.at[i, y], 7, dev(x, ys[d], z, c))

    own_wg.wait()
    own_gain.wait()
    wait(wg_recv.at[pl.ds(0, 7)], rsem.at[8])

    def scale_gain(i, carry):
        wg_buf[pl.ds(pl.multiple_of(i * 112, 112), 112)] = (wg_recv[i].astype(F32) * gain_buf[...]).astype(BF)
        return carry

    lax.fori_loop(0, NX * NC, scale_gain, 0)

    wait(xt.at[:, pl.ds(0, 3)], rsem.at[7])

    stream = xt[...].reshape(ED, TOK)
    wide = stream.astype(F32)
    squares = jnp.sum(wide * wide, axis=0, keepdims=True)
    high = squares.astype(BF).astype(F32)
    row16 = lax.broadcasted_iota(jnp.int32, (16, TOK), 0)
    both = jnp.where(row16 == 0, high, jnp.where(row16 == 1, squares - high, 0.0)).astype(BF)
    def gate_up_block(i, carry):
        kp = xs[(2, 2, 1, 1, 3, 3, 0, 0)[i]] * NC + cs[(0, 1, 0, 1, 0, 1, 1, 0)[i]]
        part = jnp.dot(
            wg_buf[pl.ds(pl.multiple_of(kp * 112, 112), 112)], stream, preferred_element_type=F32
        )
        gsend[kp, pl.ds(0, 112)] = part.astype(BF)
        gsend[kp, pl.ds(112, 16)] = both

        if i < 7:
            to = dev(xs[(2, 2, 1, 1, 3, 3, 0)[i]], y, z, cs[(0, 1, 0, 1, 0, 1, 1)[i]])
            send(gsend.at[kp], grecv.at[k], 13, to)

        return carry

    for block in range(8):
        gate_up_block(block, 0)
    grecv[k] = gsend[k]

    own_wd.wait()
    wait(wd_recv.at[pl.ds(0, NY - 1)], rsem.at[11])

    def down_block(i, carry):
        zero = jnp.zeros((HPAD - HID, 128), BF)
        tall = [
            jnp.concatenate([wd_recv[i, pl.ds(n * HID, HID)], zero], axis=0) for n in range(NZ)
        ]
        for n in range(NZ // 2):
            pair = jnp.concatenate([tall[2 * n], tall[2 * n + 1]], axis=0)
            wd_t[pl.ds(pl.multiple_of(i * 128, 128), 128), pl.ds(n * 128, 128)] = pair.T
        return carry

    lax.fori_loop(0, NY, down_block, 0)

    wait(grecv.at[pl.ds(0, 7)], rsem.at[13])
    gu = jnp.sum(grecv[...].astype(F32), axis=0)
    inv_rms = lax.rsqrt((gu[112:113] + gu[113:114]) * (1.0 / (8 * ED)) + norm_eps)
    gate = gu[:HID] * inv_rms
    up = gu[HID : 2 * HID] * inv_rms
    hidden = gate / (1.0 + jnp.exp(-gate)) * up
    ht[z] = jnp.concatenate([hidden, jnp.zeros((HPAD - HID, TOK), F32)], axis=0).astype(BF)

    def zd(d):
        return zs[d % NZ]

    def h_send(block, d, stage):
        send(ht.at[block], ht.at[block], stage, dev(x, y, zd(d), c))

    h_send(z, 5, 16)
    h_send(z, -5, 17)
    h_send(z, 1, 18)
    h_send(z, -1, 19)
    wait(ht.at[0], rsem.at[18])
    h_send(zd(-1), 1, 20)
    wait(ht.at[0], rsem.at[19])
    h_send(zd(1), -1, 21)
    wait(ht.at[0], rsem.at[16])
    h_send(zd(-5), 3, 14)
    h_send(zd(-5), 2, 14)
    h_send(zd(-5), 1, 14)
    h_send(zd(-5), -1, 14)
    wait(ht.at[0], rsem.at[17])
    h_send(zd(5), -2, 14)
    h_send(zd(5), -1, 14)
    h_send(zd(5), 1, 14)
    wait(ht.at[0], rsem.at[20])
    h_send(zd(-2), 1, 14)
    wait(ht.at[0], rsem.at[21])
    h_send(zd(2), -1, 14)
    wait(ht.at[pl.ds(0, 9)], rsem.at[14])

    gathered = ht[...].reshape(NZ * HPAD, TOK)

    def down_project(i, carry):
        yp = ys[(2, 3, 1, 0)[i]]
        down = jnp.dot(
            wd_t[pl.ds(pl.multiple_of(yp * 128, 128), 128)], gathered, preferred_element_type=F32
        )
        rs2_send[pl.ds(yp * 8, 8)] = down.astype(BF).reshape(8, 16, TOK)
        for i in (2, 1, 3):
            for l in range(NC):
                send(rs2_send.at[yp * 8 + xs[i] * 2 + cs[l]], rs2_recv.at[me], 15, dev(xs[i], yp, z, cs[l]))
        send(rs2_send.at[yp * 8 + x * 2 + cs[1]], rs2_recv.at[me], 15, dev(x, yp, z, cs[1]))

        @pl.when(yp != y)
        def _():
            send(rs2_send.at[yp * 8 + k], rs2_recv.at[me], 15, dev(x, yp, z, c))

        return carry

    for block in range(4):
        down_project(block, 0)
    rs2_recv[me] = rs2_send[y * 8 + x * 2 + c]

    @pl.when((x != y) | jnp.logical_not(owner))
    def _():
        wait(str_recv, rsem.at[12])

    wait(ysend.at[pl.ds(0, 3)], ssem.at[0])
    wait(ystat.at[pl.ds(0, 3)], ssem.at[1])
    wait(zsend.at[pl.ds(0, 15)], ssem.at[2])
    wait(zrstat.at[pl.ds(0, 15)], ssem.at[3])
    wait(att.at[pl.ds(0, 15)], ssem.at[4])
    wait(rs1_send.at[pl.ds(0, 15)], ssem.at[5])
    wait(xt.at[:, pl.ds(0, 3)], ssem.at[7])
    wait(wg_recv.at[pl.ds(0, 7)], ssem.at[8])
    wait(wo_recv.at[pl.ds(0, 3)], ssem.at[10])
    wait(wd_recv.at[pl.ds(0, 3)], ssem.at[11])
    wait(gsend.at[pl.ds(0, 7)], ssem.at[13])
    wait(ht.at[pl.ds(0, 9)], ssem.at[14])
    wait(ht.at[0], ssem.at[16])
    wait(ht.at[0], ssem.at[17])
    wait(ht.at[0], ssem.at[18])
    wait(ht.at[0], ssem.at[19])
    wait(ht.at[0], ssem.at[20])
    wait(ht.at[0], ssem.at[21])
    wait(rs2_send.at[pl.ds(0, 31)], ssem.at[15])

    @pl.when(jnp.logical_not(owner))
    def _():
        wait(rs1_send.at[0], ssem.at[5])

    @pl.when(owner)
    def _():
        wait(xt.at[pl.ds(0, 5), pl.ds(0, 3)], ssem.at[6])

    @pl.when(owner & (x != y))
    def _():
        wait(res_recv, ssem.at[9])
        wait(res_recv, ssem.at[12])

    @pl.when(owner & (x == y))
    def _():
        wait(str_recv, ssem.at[12])

    wait(rs2_recv.at[pl.ds(0, 31)], rsem.at[15])
    result = str_recv[...].astype(F32) + jnp.sum(rs2_recv[...].astype(F32), axis=0)
    rounded = result.astype(BF)
    out_ref[0] = rounded[:, :REQ]
    out_ref[1] = rounded[:, REQ:]


def body(
    resid,
    queries,
    new_kv,
    prefix_cache,
    suffix_cache,
    suffix_lengths,
    out_weight,
    norm_gain,
    gate_up,
    down_weight,
):
    hbm = pl.BlockSpec(memory_space=pl.ANY)
    vmem = pltpu.VMEM
    in_vmem = pl.BlockSpec(memory_space=vmem)
    result = pl.pallas_call(
        kernel,
        out_shape=jax.ShapeDtypeStruct((2, 16, REQ), BF),
        in_specs=[hbm] * 10,
        out_specs=in_vmem,
        scratch_shapes=[
            vmem((1, REQ), jnp.int32), vmem((2, 2, DH), BF), vmem((TOK, 128), BF),
            vmem((TOK, HEADS, DH), BF), vmem((TOK * HEADS, DH), F32), vmem((NY, DH, 2 * TOK), BF),
            vmem((KEYS, DH), BF), vmem((KEYS, DH), BF), vmem((DH, KEYS), BF), vmem((2, 8, DH), F32),
            vmem((128, TOK), BF),
            vmem((NY, 256, TOK), BF), vmem((NY, 4, TOK), F32), vmem((NY, 256, TOK), BF), vmem((NY, 4, TOK), F32),
            vmem((NZ, 16, TOK), BF), vmem((2, 1, TOK), F32), vmem((NZ, 16, TOK), BF), vmem((NZ, 1, TOK), F32),
            vmem((NZ, 16, TOK), BF),
            vmem((NY, 256, 128), BF), vmem((512, 256), BF), vmem((16, 32, TOK), BF), vmem((32, 32, TOK), BF),
            vmem((32, TOK), BF),
            vmem((8, NY, 32, TOK), BF), vmem((8, 112, ED), BF), vmem((8 * 112, ED), BF), vmem((1, ED), F32),
            vmem((8, 128, TOK), BF), vmem((8, 128, TOK), BF),
            vmem((NZ, HPAD, TOK), BF), vmem((NY, 896, 128), BF), vmem((512, NZ * HPAD), BF),
            vmem((32, 16, TOK), BF), vmem((32, 16, TOK), BF), vmem((16, TOK), BF),
            pltpu.SemaphoreType.DMA((12,)), pltpu.SemaphoreType.DMA((22,)), pltpu.SemaphoreType.DMA((SX + 8,)),
        ],
        compiler_params=pltpu.CompilerParams(
            collective_id=0, has_side_effects=True, vmem_limit_bytes=63 * 1024 * 1024
        ),
        name="layer",
    )(
        suffix_lengths.reshape(1, REQ), new_kv[:, 0, :, 0, :], resid.reshape(TOK, 128),
        queries.reshape(TOK, HEADS, DH), prefix_cache[:, :, 0, :], suffix_cache[:, 0, :, 0, :],
        out_weight, norm_gain.reshape(8, 1, ED), gate_up[:, :, 0, :].transpose(0, 2, 1).reshape(2 * HID, 8 * ED),
        down_weight,
    )
    return result.transpose(2, 0, 1)


def solution(mesh):
    placed = (
        P(None, None, "seq"),
        P(None, None, "kvh", None),
        P(None, "seq", None, "kvh", None),
        P(None, "seq", "kvh", None),
        P(None, "seq", None, "kvh", None),
        P(),
        P("kvh", "seq"),
        P(),
        P(None, None, "kvh", "seq"),
        P("kvh", "seq"),
    )
    return jax.shard_map(
        body, mesh=mesh, in_specs=placed, out_specs=P(None, None, ("seq", "kvh")), check_vma=False
    )
```
